256 devices in a mesh: img: 4 (over y_lo, core), cls: 64 (over x, z, y_hi).
Axes of the slice: x: 4, y: 4 (y_hi: 2, y_lo: 2; y = y_hi * 2 + y_lo), z: 8, core: 2. Of those that a mesh axis runs over, the one named last changes fastest.
Arguments:
- images: bfloat16 [16384, 4096], P(('img', 'cls')), may hold values from -64 to 64
- noise_var: float32 [16384], P(('img', 'cls')), may hold values from 16 to 128
- references: bfloat16 [256, 4096], P('cls'), may hold values from -3.5 to 3.5
- assign: int32 [16384, 4], P(('img', 'cls')), may hold values from 0 to 255, all different within a row; in each aligned block of 64 rows (0 to 63, 64 to 127, ...) at most 6 rows name the same one
- rotations: int32 [16384, 4], P(('img', 'cls')), may hold values from 0 to 7
Outputs:
- new_references: float32 [256, 4096], P('cls')
- log_evidence: float32 [16384], P(('img', 'cls'))
The draws below stay inside these ranges and needn't reach their ends.
Inputs may be any that keep to these rules, and one draw needn't show every extreme that they name: `assign`: the candidates of one image are different classes. Within the rows of one device (aligned blocks of 64 rows) no class is named by more than 6 entries, and every class is named somewhere.
All inputs are finite; a program needn't handle non-finite values.
Results may differ from the reference program's by a relative error of at most 0.00085.
Values may be sent and summed in bfloat16 or wider, within the bound.
A program may use at most 128 MiB of HBM per device.

```python
import math
import jax
import jax.numpy as jnp
import numpy as np
from jax import lax

SIDE = 64
K = 256
CANDS = 4
MOST = 6
IMG_DEV = 64
NIMG = 16384


def shared_references(key):
    sub = jax.random.fold_in(key, 901)
    values = jax.random.normal(sub, (K, SIDE * SIDE), jnp.float32)
    return jnp.clip(values, -3.5, 3.5)


def shared_variance(key):
    sub = jax.random.fold_in(key, 902)
    level = jax.random.uniform(sub, (NIMG,), jnp.float32)
    return 16.0 * jnp.exp(level * math.log(8.0))


def draw_references(key, part):
    return shared_references(key).astype(jnp.bfloat16)


def draw_noise_var(key, part):
    return shared_variance(key)


def draw_images(key, part):
    pixels = SIDE * SIDE
    key = jax.random.fold_in(key, 3)
    values = jnp.clip(jax.random.normal(key, (NIMG, pixels), jnp.float32), -6.0, 6.0)
    return values.astype(jnp.bfloat16)


def with_ends(array, key, smallest, top_value):
    extent = array.shape
    place = [jax.random.randint(jax.random.fold_in(key, axis), (), 0, extent[axis]) for axis in range(len(extent))]
    array = array.at[tuple(place)].set(smallest)
    longest = extent.index(max(extent))
    place[longest] = (place[longest] + 1) % extent[longest]
    return array.at[tuple(place)].set(top_value)


def routed_block(rng, own, number, rows, count, top, most, skew):
    ranking = jax.random.permutation(rng, count)
    packed, ordinary = shares(count, rows * top, most, skew, True), shares(count, rows * top, most, skew, False)
    places = jnp.arange(count)

    def named(lengths, rotation):
        used = int((lengths > 0).sum())
        fixed = max(1, used // 4)
        passed = fixed + (places - fixed + rotation * (used - fixed)) % max(1, count - fixed)
        return jnp.zeros((count,), jnp.int32).at[ranking[jnp.where(places < fixed, places, passed)]].set(jnp.asarray(lengths, jnp.int32))

    lengths = jnp.where(number % 4 == 0, named(packed, number // 4), named(ordinary, number - number // 4 - 1))
    mixed = jax.random.permutation(jax.random.fold_in(own, 3), count)
    source_of, receiver = mixed[0:count // 2 * 2:2], mixed[1:count // 2 * 2:2]
    slack = jnp.minimum(lengths[source_of] - 1, most - lengths[receiver]) // 2
    slack = jnp.where((source_of == ranking[0]) | (receiver == ranking[0]) | (lengths[receiver] == 0), 0, jnp.maximum(slack, 0))
    passed = jax.random.randint(jax.random.fold_in(own, 4), (count // 2,), 0, 1 << 20) % (slack + 1)
    lengths = lengths.at[source_of].add(-passed).at[receiver].add(passed)
    items = jnp.searchsorted(jnp.cumsum(lengths), jnp.arange(rows * top), side="right").astype(jnp.int32)
    grid = items.reshape(top, rows).T
    grid = grid[jax.random.permutation(jax.random.fold_in(own, 1), rows)]
    rotation = jax.random.randint(jax.random.fold_in(own, 2), (rows, 1), 0, top)
    return jnp.take_along_axis(grid, (jnp.arange(top)[None, :] + rotation) % top, axis=1)


def shares(number_of, total, bound, skew, full):
    weights = [(1 << 20) // math.isqrt(rank ** skew) + 1 for rank in range(1, number_of + 1)]
    largest = bound if full else min(bound, max(-(-total // number_of), total * weights[0] // sum(weights)))
    least = 1 if total - largest >= number_of - 1 else 0
    counts, rest = [largest] + [least] * (number_of - 1), total - largest - least * (number_of - 1)
    while rest > 0:
        candidates = [i for i in range(1, number_of) if counts[i] < largest] or [i for i in range(1, number_of) if counts[i] < bound]
        whole, remaining = sum([weights[i] for i in candidates]), rest
        for i in candidates:
            addition = min(bound - counts[i], max(1, remaining * weights[i] // whole), rest)
            counts[i] = counts[i] + addition
            rest = rest - addition
    return np.array(counts)


def setup_inputs(seed: int = 0) -> dict:
    splits = jax.random.split(jax.random.key(seed), 6)
    images = draw_images(jax.random.fold_in(splits[5], 71), 0)
    noise_var = draw_noise_var(jax.random.fold_in(splits[5], 71), 0)
    references = draw_references(jax.random.fold_in(splits[5], 71), 0)
    assign_keys = jax.random.split(jax.random.fold_in(splits[3], 1), NIMG // IMG_DEV)
    assign_turns = jax.random.permutation(jax.random.fold_in(splits[3], 3), NIMG // IMG_DEV)
    assign = jax.vmap(lambda own, number: routed_block(jax.random.fold_in(splits[3], 2), own, number, IMG_DEV, K, CANDS, MOST, 1))(assign_keys, assign_turns).reshape((NIMG, CANDS))
    rotations = with_ends(jax.random.randint(splits[4], (NIMG, CANDS), 0, 8), jax.random.fold_in(splits[4], 1), 0, 7).astype(jnp.int32)
    return dict(images=images, noise_var=noise_var, references=references, assign=assign, rotations=rotations)


prior_weight = 16.0


def forward_turn(pictures, turn):
    quarter = turn % 4
    if turn >= 4:
        pictures = jnp.swapaxes(pictures, -1, -2)
    return jnp.rot90(pictures, quarter, axes=(-2, -1))


def backward_turn(pictures, turn):
    quarter = turn % 4
    result = jnp.rot90(pictures, -quarter, axes=(-2, -1))
    if turn >= 4:
        result = jnp.swapaxes(result, -1, -2)
    return result


def reference(images, noise_var, references, assign, rotations):
    pixels = SIDE * SIDE
    squares = references.reshape(K, SIDE, SIDE)
    turned_refs = jnp.concatenate([forward_turn(squares, t).reshape(K, pixels) for t in range(8)], axis=0)
    norms = jnp.sum(jnp.square(references.astype(jnp.float32)), axis=1)
    blocks = NIMG // IMG_DEV
    inputs = (images.reshape(blocks, IMG_DEV, pixels), noise_var.reshape(blocks, IMG_DEV),
              assign.reshape(blocks, IMG_DEV, CANDS), rotations.reshape(blocks, IMG_DEV, CANDS))

    def step(carry, block):
        sums, totals = carry
        pics, variance, chosen, turns = block
        raw = jnp.dot(pics, turned_refs.T, preferred_element_type=jnp.float32).reshape(IMG_DEV, 8, K)
        scores = (raw - 0.5 * norms[None, None, :]) / variance[:, None, None]
        peak = jnp.max(scores, axis=(1, 2))
        evidence = peak + jnp.log(jnp.sum(jnp.exp(scores - peak[:, None, None]), axis=(1, 2)))
        top = jnp.max(scores, axis=1)
        per_class = top + jnp.log(jnp.sum(jnp.exp(scores - top[:, None, :]), axis=1))
        candidate = jnp.take_along_axis(per_class, chosen, axis=1)
        best = jnp.max(candidate, axis=1, keepdims=True)
        expo = jnp.exp(candidate - best)
        weights = (expo / jnp.sum(expo, axis=1, keepdims=True)).astype(jnp.bfloat16)
        square_pics = pics.reshape(IMG_DEV, SIDE, SIDE)
        reverted = jnp.stack([backward_turn(square_pics, t).reshape(IMG_DEV, pixels) for t in range(8)], axis=0)
        aligned = reverted[turns, jnp.arange(IMG_DEV)[:, None]]
        weighted = weights.astype(jnp.float32)[:, :, None] * aligned.astype(jnp.float32)
        labels = chosen.reshape(-1)
        sums = sums + jax.ops.segment_sum(weighted.reshape(-1, pixels), labels, num_segments=K)
        totals = totals + jax.ops.segment_sum(weights.astype(jnp.float32).reshape(-1), labels, num_segments=K)
        return (sums, totals), evidence

    start = (jnp.zeros((K, pixels), jnp.float32), jnp.zeros((K,), jnp.float32))
    (sums, totals), evidence = lax.scan(step, start, inputs)
    updated = (sums + prior_weight * references.astype(jnp.float32)) / (totals + prior_weight)[:, None]
    return updated, evidence.reshape(NIMG)
```

```python
import jax
import jax.numpy as jnp
from jax import lax
from jax.sharding import PartitionSpec as P

SIDE = 64
K = 256

prior_weight = 16.0


def backward_turn(pictures, turn):
    quarter = turn % 4
    result = jnp.rot90(pictures, -quarter, axes=(-2, -1))
    if turn >= 4:
        result = jnp.swapaxes(result, -1, -2)
    return result


def per_device(images, noise_var, references, assign, rotations):
    count, pixels = images.shape
    square_pics = images.reshape(count, SIDE, SIDE)
    reverted = jnp.concatenate(
        [backward_turn(square_pics, t).reshape(count, pixels) for t in range(8)], axis=0
    )
    piece = lax.all_gather(references, "cls", axis=0, tiled=True)
    norms = jnp.sum(jnp.square(piece.astype(jnp.float32)), axis=1)
    raw = jnp.einsum("np,kp->nk", reverted, piece, preferred_element_type=jnp.float32).reshape(
        8, count, K
    )
    scores = (raw - 0.5 * norms[None, None, :]) / noise_var[None, :, None]
    top = jnp.max(scores, axis=0)
    per_class = top + jnp.log(jnp.sum(jnp.exp(scores - top[None]), axis=0))
    peak = jnp.max(per_class, axis=1, keepdims=True)
    log_evidence = (peak + jnp.log(jnp.sum(jnp.exp(per_class - peak), axis=1, keepdims=True)))[:, 0]
    labels = jnp.arange(K, dtype=jnp.int32)
    match = assign[:, :, None] == labels[None, None, :]
    candidate = jnp.sum(jnp.where(match, per_class[:, None, :], 0.0), axis=2)
    best = jnp.max(candidate, axis=1, keepdims=True)
    expo = jnp.exp(candidate - best)
    weights = (expo / jnp.sum(expo, axis=1, keepdims=True)).astype(jnp.bfloat16)
    spread = jnp.where(match, weights[:, :, None], 0)
    turns = rotations[None] == jnp.arange(8, dtype=jnp.int32)[:, None, None]
    table = jnp.sum(jnp.where(turns[..., None], spread[None], 0), axis=2).reshape(8 * count, K)
    sums = jnp.einsum("nk,np->kp", table, reverted, preferred_element_type=jnp.float32)
    totals = jnp.sum(spread.astype(jnp.float32), axis=(0, 1))
    sums, totals = lax.psum_scatter((sums, totals), "cls", scatter_dimension=0, tiled=True)
    sums, totals = lax.psum((sums, totals), "img")
    updated = (sums + prior_weight * references.astype(jnp.float32)) / (totals + prior_weight)[
        :, None
    ]
    return (updated, log_evidence)


def solution(mesh):
    in_specs = (
        P(("img", "cls"), None),
        P(("img", "cls")),
        P("cls", None),
        P(("img", "cls"), None),
        P(("img", "cls"), None),
    )
    out_specs = (P("cls", None), P(("img", "cls")))
    return jax.shard_map(
        per_device, mesh=mesh, in_specs=in_specs, out_specs=out_specs, check_vma=False
    )
```

```python
import functools

import numpy as np
import jax
import jax.numpy as jnp
from jax import lax
from jax.experimental import pallas as pl
from jax.experimental.pallas import tpu as pltpu
from jax.sharding import PartitionSpec as P

SIDE = 64
K = 256
PIXELS = SIDE * SIDE
MESH = pl.DeviceIdType.MESH
F32 = jnp.float32
BF16 = jnp.bfloat16
prior_weight = 16.0

HALVES = (
    ((0, 0), (0, 3), (3, 0), (3, 3), (1, 1), (1, 2), (2, 1), (2, 2)),
    ((0, 1), (0, 2), (3, 1), (3, 2), (1, 0), (2, 0), (1, 3), (2, 3)),
)


def backward_turn(picture, turn):
    quarter = turn % 4
    result = np.rot90(picture, -quarter, axes=(-2, -1))
    return np.swapaxes(result, -1, -2) if turn >= 4 else result


def tables():
    number = np.arange(PIXELS).reshape(SIDE, SIDE)
    inner = np.zeros((8, 256, 256), np.float32)
    moves = []
    for r in range(8):
        source = backward_turn(number, r)
        per_half = []
        for half in HALVES:
            row = []
            for bi, bj in half:
                piece = source[bi * 16:bi * 16 + 16, bj * 16:bj * 16 + 16].reshape(-1)
                i, j = piece // SIDE, piece % SIDE
                row.append(half.index((int(i[0]) // 16, int(j[0]) // 16)))
                inner[r, (i % 16) * 16 + j % 16, np.arange(256)] = 1.0
            per_half.append(row)
        assert (inner[r].sum(axis=0) == 1).all() and (inner[r].sum(axis=1) == 1).all()
        moves.append(per_half)
    regroup = np.zeros((4, 1024, 256), np.float32)
    for bj in range(4):
        for ii in range(16):
            for jj in range(16):
                regroup[bj, ii * 64 + bj * 16 + jj, ii * 16 + jj] = 1.0
    return moves, inner, regroup


MOVES, INNER, REGROUP = tables()


def wrap(value, size):
    return lax.rem(value + 2 * size, size)


def kernel(X, Z, images_hbm, refs_ref, meta_ref, inner_hbm, regroup_hbm, out_ref, evidence_ref,
           im, inner, regroup, blocks, xall, turned, meta, ref_slab, zgot, zline, refs, own_scores, other_scores,
           per_class, table, part, got_a, got_b, got_a2, got_b2, tot, tot_y, tot_x, zsend, zrecv, slots, lines,
           local_sem, send_sem, recv_sem):
    img, cls = lax.axis_index("img"), lax.axis_index("cls")
    yl, h = img // 2, lax.rem(img, 2)
    yh, z, x = lax.rem(cls, 2), lax.rem(cls // 2, Z), cls // (2 * Z)
    y = yh * 2 + yl

    def device(x_, y_, z_, h_):
        return {"img": lax.rem(y_, 2) * 2 + h_, "cls": (x_ * Z + z_) * 2 + y_ // 2}

    other_core = device(x, y, z, 1 - h)
    along_x = [device(wrap(x + d, X), y, z, h) for d in range(1, 4)]
    along_y = [device(x, wrap(y + d, 4), z, h) for d in range(1, 4)]
    along_z = [device(x, y, wrap(z + d, Z), h) for d in range(1, Z)]
    mate_y = yh * 2 + 1 - yl
    replicas = [other_core, device(x, mate_y, z, h), device(x, mate_y, z, 1 - h)]

    barrier = pltpu.get_barrier_semaphore()
    partners = [other_core] + along_x + along_y + along_z + [replicas[2]]
    for partner in partners:
        pl.semaphore_signal(barrier, inc=1, device_id=partner, device_id_type=MESH)

    fetch = [
        pltpu.make_async_copy(regroup_hbm, regroup, local_sem.at[0]),
        pltpu.make_async_copy(images_hbm, im, local_sem.at[1]),
        pltpu.make_async_copy(inner_hbm, inner, local_sem.at[2]),
    ]
    for copy in fetch:
        copy.start()

    count = [0]
    sent = []

    def new_id():
        count[0] += 1
        return count[0] - 1

    def send(src, dst, ident, to):
        copy = pltpu.make_async_remote_copy(src_ref=src, dst_ref=dst, send_sem=send_sem.at[ident],
                                            recv_sem=recv_sem.at[ident], device_id=to, device_id_type=MESH)
        copy.start()
        sent.append(copy)

    def arrived(dst, ident):
        pltpu.make_async_remote_copy(src_ref=dst, dst_ref=dst, send_sem=send_sem.at[ident],
                                     recv_sem=recv_sem.at[ident], device_id=other_core,
                                     device_id_type=MESH).wait_recv()

    fetch[0].wait()
    for b in range(4):
        v = [[HALVES[hh][q * 4 + b] for q in range(2)] for hh in range(2)]
        bi, bj = [v[0][0][a] + h * (v[1][0][a] - v[0][0][a]) + yl * (v[0][1][a] - v[0][0][a])
                  + h * yl * (v[1][1][a] - v[1][0][a] - v[0][1][a] + v[0][0][a]) for a in range(2)]
        strip = refs_ref[:, pl.ds(pl.multiple_of(bi * 1024, 1024), 1024)]
        ref_slab[b * 4:b * 4 + 4, :] = jnp.dot(strip, regroup[bj], preferred_element_type=F32)
    zgot[z] = ref_slab[...].astype(BF16)

    pl.semaphore_wait(barrier, len(partners))

    ident_z = [new_id() for _ in range(Z - 1)]
    for d in range(1, Z):
        send(zgot.at[z], zgot.at[z], ident_z[d - 1], along_z[d - 1])
    ident_meta, ident_im = new_id(), new_id()
    meta[h] = meta_ref[...]
    send(meta.at[h], meta.at[h], ident_meta, other_core)

    fetch[1].wait()
    for hh in range(2):
        for b, (bi, bj) in enumerate(HALVES[hh]):
            blocks[hh * 8 + b] = jnp.dot(im[:, bi * 1024:bi * 1024 + 1024], regroup[bj],
                                         preferred_element_type=F32).astype(BF16)
    mine = pl.ds(pl.multiple_of(h * 64, 64), 64)
    theirs = pl.ds(pl.multiple_of((1 - h) * 64, 64), 64)
    send(blocks.at[pl.ds((1 - h) * 8, 8)], xall.at[:, mine, :], ident_im, other_core)
    for b in range(8):
        xall[b, mine, :] = blocks[h * 8 + b]

    for d in range(1, Z):
        arrived(zgot.at[wrap(z - d, Z)], ident_z[d - 1])

    def rows(x_, y_):
        return pl.ds(pl.multiple_of((y_ // 2) * 128 + x_ * 32, 32), 32)

    def region(ref, part_, x_, y_):
        return ref.at[pl.ds(lax.rem(y_, 2) * 4 + part_ * 2, 2), rows(x_, y_), :]

    for q in range(Z):
        piece = zgot[q].astype(F32)
        for b in range(4):
            zline[b, q * 4:q * 4 + 4, :] = piece[b * 4:b * 4 + 4, :]
    for b in range(4):
        refs[yl * 4 + b, rows(x, y), :] = zline[b].astype(BF16)

    first_a, first_b = [new_id() for _ in range(3)], [new_id() for _ in range(3)]
    second_a = [[new_id() for _ in range(3)] for _ in range(4)]
    second_b = [[new_id() for _ in range(3)] for _ in range(4)]
    for d in range(3):
        send(region(refs, 0, x, y), region(refs, 0, x, y), first_a[d], along_x[d])
        send(region(refs, 1, x, y), region(refs, 1, x, y), first_b[d], along_y[d])
    for e in range(4):
        xe, ye = wrap(x - e, X), wrap(y - e, 4)
        if e:
            arrived(region(refs, 0, xe, y), first_a[e - 1])
        for d in range(3):
            send(region(refs, 0, xe, y), region(refs, 0, xe, y), second_a[e][d], along_y[d])
        if e:
            arrived(region(refs, 1, x, ye), first_b[e - 1])
        for d in range(3):
            send(region(refs, 1, x, ye), region(refs, 1, x, ye), second_b[e][d], along_x[d])

    fetch[2].wait()
    arrived(xall.at[:, theirs, :], ident_im)
    for r in range(8):
        for b in range(8):
            p0, p1 = MOVES[r][0][b], MOVES[r][1][b]
            turned[b, r * 128:r * 128 + 128, :] = jnp.dot(
                xall[p0 + h * (p1 - p0)], inner[r], preferred_element_type=F32).astype(BF16)

    arrived(meta.at[1 - h], ident_meta)
    lane = lax.broadcasted_iota(jnp.int32, (16, 128), 1)
    info = jnp.where(lane < 64, meta[0], meta[1])
    kappa = lax.broadcasted_iota(jnp.int32, (K, 128), 0)
    label = (((kappa >> 2) & 31) * 8 + (kappa >> 7) * 4 + (kappa & 3)).astype(F32)
    tie = jnp.full((K, 128), -1.0, F32)
    for j in range(4):
        tie = jnp.where(label == info[1 + j:2 + j, :], info[5 + j:6 + j, :], tie)
    per_noise = 1.0 / info[0:1, :]

    for e in range(4):
        for d in range(3):
            arrived(region(refs, 0, wrap(x - e, X), wrap(y - d - 1, 4)), second_a[e][d])
            arrived(region(refs, 1, wrap(x - d - 1, X), wrap(y - e, 4)), second_b[e][d])

    square = jnp.zeros((K, 128), F32)
    for b in range(8):
        part_ref = refs[b].astype(F32)
        sq = part_ref * part_ref
        square = square + sq[:, :128] + sq[:, 128:]
    half_norm = 0.5 * jnp.sum(square, axis=1, keepdims=True)
    ident_s = [new_id() for _ in range(4)]
    for c in range(4):
        acc = jnp.zeros((K, 256), F32)
        for b in range(8):
            acc = acc + lax.dot_general(refs[b], turned[b, c * 256:c * 256 + 256, :], (((1,), (1,)), ((), ())),
                                        preferred_element_type=F32)
        own_scores[c] = acc - half_norm
        send(own_scores.at[c], other_scores.at[c], ident_s[c], other_core)
    for c in range(4):
        arrived(other_scores.at[c], ident_s[c])

    @pl.loop(0, 8)
    def _(i):
        row = pl.ds(pl.multiple_of(i * 32, 32), 32)
        score = []
        for c in range(4):
            both = own_scores[c, row, :] + other_scores[c, row, :]
            score += [both[:, :128] * per_noise, both[:, 128:] * per_noise]
        top = score[0]
        for s in score[1:]:
            top = jnp.maximum(top, s)
        total = jnp.exp(score[0] - top)
        for s in score[1:]:
            total = total + jnp.exp(s - top)
        per_class[row, :] = top + jnp.log(total)

    value = per_class[...]
    peak = jnp.max(value, axis=0, keepdims=True)
    evidence = peak + jnp.log(jnp.sum(jnp.exp(value - peak), axis=0, keepdims=True))
    evidence = jnp.broadcast_to(evidence, (8, 128))
    evidence_ref[...] = jnp.where(h == 0, evidence, pltpu.roll(evidence, 64, 1))
    named = tie >= 0.0
    best = jnp.max(jnp.where(named, value, -jnp.inf), axis=0, keepdims=True)
    expo = jnp.where(named, jnp.exp(jnp.where(named, value, best) - best), 0.0)
    weight = (expo / jnp.sum(expo, axis=0, keepdims=True)).astype(BF16).astype(F32)
    for r in range(8):
        table[:, r * 128:r * 128 + 128] = jnp.where(tie == r, weight, 0.0).astype(BF16)
    tot[...] = lax.dot_general(jnp.ones((8, 128), BF16), weight.astype(BF16), (((1,), (1,)), ((), ())),
                               preferred_element_type=F32)

    ident_ty, ident_tx = [new_id() for _ in range(3)], [new_id() for _ in range(3)]
    for d in range(3):
        send(tot, tot_y.at[d], ident_ty[d], along_y[d])
    one_a = [[new_id() for _ in range(4)] for _ in range(3)]
    one_b = [[new_id() for _ in range(4)] for _ in range(3)]
    two_a, two_b = [new_id() for _ in range(3)], [new_id() for _ in range(3)]
    for turn in range(2):
        quad = (1 - yl) * (1 - turn) + yl * turn
        for b in range(4):
            part[quad * 4 + b] = jnp.dot(table[...], turned[quad * 4 + b], preferred_element_type=F32)
        for e in (1, 2, 3, 0):
            for d in ((1, 3), (2,))[turn]:
                yd = wrap(y + d, 4)
                send(region(part, 0, wrap(x + e, X), yd), got_a.at[d - 1, e], one_a[d - 1][e], along_y[d - 1])
            if e in ((1, 3), (2, 0))[turn]:
                for d in (1, 2, 3):
                    xd = wrap(x + d, X)
                    send(region(part, 1, xd, wrap(y + e, 4)), got_b.at[d - 1, e], one_b[d - 1][e], along_x[d - 1])

    for d in range(3):
        arrived(tot_y.at[d], ident_ty[d])
    lines[...] = tot[...] + tot_y[0] + tot_y[1] + tot_y[2]
    for d in range(3):
        send(lines, tot_x.at[d], ident_tx[d], along_x[d])

    for e in (1, 3, 2, 0):
        for d in range(3):
            arrived(got_a.at[d, e], one_a[d][e])
        mine_a = region(part, 0, wrap(x + e, X), y)
        mine_a[...] = mine_a[...] + got_a[0, e] + got_a[1, e] + got_a[2, e]
        if e:
            send(mine_a, got_a2.at[e - 1], two_a[e - 1], along_x[e - 1])
        for d in range(3):
            arrived(got_b.at[d, e], one_b[d][e])
        mine_b = region(part, 1, x, wrap(y + e, 4))
        mine_b[...] = mine_b[...] + got_b[0, e] + got_b[1, e] + got_b[2, e]
        if e:
            send(mine_b, got_b2.at[e - 1], two_b[e - 1], along_y[e - 1])

    for d in range(3):
        arrived(tot_x.at[d], ident_tx[d])
    line = lines[...] + tot_x[0] + tot_x[1] + tot_x[2]
    for two, got, p in ((two_a, got_a2, 0), (two_b, got_b2, 1)):
        for d in range(3):
            arrived(got.at[d], two[d])
        whole = region(part, p, x, y)[...] + got[0] + got[1] + got[2]
        for b in range(2):
            for q in range(Z):
                zsend[q, (p * 2 + b) * 4:(p * 2 + b) * 4 + 4, :] = whole[b, q * 4:q * 4 + 4, :]
    for q in range(Z):
        zsend[q, 16:24, :] = line
    ident_zr = [new_id() for _ in range(Z - 1)]
    for d in range(1, Z):
        send(zsend.at[wrap(z + d, Z)], zrecv.at[d - 1], ident_zr[d - 1], along_z[d - 1])
    final = zsend[z]
    for d in range(Z - 1):
        arrived(zrecv.at[d], ident_zr[d])
        final = final + zrecv[d]
    place = lax.broadcasted_iota(jnp.int32, (16, 256), 1)
    own_class = yh * 128 + x * 32 + z * 4 + (lax.broadcasted_iota(jnp.int32, (16, 256), 0) & 3)
    total = jnp.sum(jnp.where(place == own_class, jnp.broadcast_to(final[16:17, :], (16, 256)), 0.0), axis=1,
                    keepdims=True)
    slots[img] = (final[:16, :] + prior_weight * ref_slab[...]) / (total + prior_weight)

    ident_o = [new_id() for _ in range(3)]
    partner_img = (yl * 2 + 1 - h, (1 - yl) * 2 + h, (1 - yl) * 2 + 1 - h)
    for d in range(3):
        send(slots.at[img], slots.at[img], ident_o[d], replicas[d])
    for d in range(3):
        arrived(slots.at[partner_img[d]], ident_o[d])
    natural = jnp.zeros((16, 1024), F32)
    for bj in range(4):
        for bi in range(4):
            hh = 0 if (bi, bj) in HALVES[0] else 1
            at = HALVES[hh].index((bi, bj))
            zline[0, bi * 4:bi * 4 + 4, :] = slots[(at // 4) * 2 + hh, (at % 4) * 4:(at % 4) * 4 + 4, :]
        left = zline[0, 0:16, :]
        for _ in range(3):
            high = left.astype(BF16)
            left = left - high.astype(F32)
            natural = natural + lax.dot_general(high, regroup[bj], (((1,), (1,)), ((), ())),
                                                preferred_element_type=F32)
    for bi in range(4):
        out_ref[:, bi * 1024:bi * 1024 + 1024] = natural[bi * 4:bi * 4 + 4, :]

    for copy in sent:
        copy.wait_send()
    assert count[0] <= send_sem.shape[0]


def per_device(images, noise_var, references, assign, rotations):
    count = images.shape[0]
    owners = lax.axis_size("cls")
    X, Z = 4, owners // 8
    info = jnp.concatenate([noise_var[None, :], assign.T.astype(F32), rotations.T.astype(F32),
                            jnp.ones((7, count), F32)], axis=0)
    info = jnp.concatenate([info, info], axis=1)
    vmem, anywhere = pl.BlockSpec(memory_space=pltpu.VMEM), pl.BlockSpec(memory_space=pl.ANY)
    out, evidence = pl.pallas_call(
        functools.partial(kernel, X, Z),
        out_shape=(jax.ShapeDtypeStruct((4, PIXELS), F32), jax.ShapeDtypeStruct((8, 128), F32)),
        in_specs=[anywhere, vmem, vmem, anywhere, anywhere],
        out_specs=(vmem, vmem),
        scratch_shapes=[
            pltpu.VMEM((count, PIXELS), BF16),
            pltpu.VMEM((8, 256, 256), BF16),
            pltpu.VMEM((4, 1024, 256), BF16),
            pltpu.VMEM((16, count, 256), BF16),
            pltpu.VMEM((8, 2 * count, 256), BF16),
            pltpu.VMEM((8, 1024, 256), BF16),
            pltpu.VMEM((2, 16, 128), F32),
            pltpu.VMEM((16, 256), F32),
            pltpu.VMEM((Z, 16, 256), BF16),
            pltpu.VMEM((4, 32, 256), F32),
            pltpu.VMEM((8, K, 256), BF16),
            pltpu.VMEM((4, K, 256), F32),
            pltpu.VMEM((4, K, 256), F32),
            pltpu.VMEM((K, 128), F32),
            pltpu.VMEM((K, 1024), BF16),
            pltpu.VMEM((8, K, 256), F32),
            pltpu.VMEM((3, 4, 2, 32, 256), F32),
            pltpu.VMEM((3, 4, 2, 32, 256), F32),
            pltpu.VMEM((3, 2, 32, 256), F32),
            pltpu.VMEM((3, 2, 32, 256), F32),
            pltpu.VMEM((8, 256), F32),
            pltpu.VMEM((3, 8, 256), F32),
            pltpu.VMEM((3, 8, 256), F32),
            pltpu.VMEM((Z, 24, 256), F32),
            pltpu.VMEM((Z - 1, 24, 256), F32),
            pltpu.VMEM((4, 16, 256), F32),
            pltpu.VMEM((8, 256), F32),
            pltpu.SemaphoreType.DMA((3,)),
            pltpu.SemaphoreType.DMA((96,)),
            pltpu.SemaphoreType.DMA((96,)),
        ],
        compiler_params=pltpu.CompilerParams(collective_id=0, has_side_effects=True, vmem_limit_bytes=48 << 20),
        name="classify",
    )(images, references, info, jnp.asarray(INNER, BF16), jnp.asarray(REGROUP, BF16))
    return out, evidence[0, :count]


def solution(mesh):
    in_specs = (
        P(("img", "cls"), None),
        P(("img", "cls")),
        P("cls", None),
        P(("img", "cls"), None),
        P(("img", "cls"), None),
    )
    out_specs = (P("cls", None), P(("img", "cls")))
    return jax.shard_map(
        per_device, mesh=mesh, in_specs=in_specs, out_specs=out_specs, check_vma=False
    )
```

```python
import functools

import numpy as np
import jax
import jax.numpy as jnp
from jax import lax
from jax.experimental import pallas as pl
from jax.experimental.pallas import tpu as pltpu
from jax.sharding import PartitionSpec as P

SIDE = 64
K = 256
MESH = pl.DeviceIdType.MESH
F32 = jnp.float32
BF16 = jnp.bfloat16
prior_weight = 16.0

STRIP = ((0, 3), (1, 2))
FLIP_ROWS, FLIP_COLUMNS = 188, 67


def backward_turn(picture, turn):
    quarter = turn % 4
    result = np.rot90(picture, -quarter, axes=(-2, -1))
    return np.swapaxes(result, -1, -2) if turn >= 4 else result


def forms():
    number = np.arange(SIDE * SIDE).reshape(SIDE, SIDE)
    found = []
    for r in range(8):
        source = backward_turn(number, r)
        for swap in (0, 1):
            for rows in (0, 1):
                for columns in (0, 1):
                    trial = number.T if swap else number
                    trial = trial[::-1] if rows else trial
                    trial = trial[:, ::-1] if columns else trial
                    if (trial == source).all():
                        found.append((swap, rows * FLIP_ROWS ^ columns * FLIP_COLUMNS))
    assert len(found) == 8
    return found


FORMS = forms()


def wrap(value, size):
    return lax.rem(value + 2 * size, size)


def kernel(X, Z, images_hbm, refs_ref, noise_ref, assign_ref, turn_ref, out_ref, evidence_ref,
           im, inner, regroup, blocks, xall, xquad, turned, turned_quad, meta, ref_slab, zgot, zline, refs, own_scores,
           other_scores, per_class, tie, table, part, got_a, got_b, got_a2, got_b2, wts, tot, tot_y, tot_x, lines, zsend,
           zrecv, leave, slots, local_sem, send_sem, recv_sem):
    img, cls = lax.axis_index("img"), lax.axis_index("cls")
    yl, h = img // 2, lax.rem(img, 2)
    yh, z, x = lax.rem(cls, 2), lax.rem(cls // 2, Z), cls // (2 * Z)
    y = yh * 2 + yl
    xp, xb = x // 2, lax.rem(x, 2)
    xm, ym, xr, yr = x + 1 - 2 * xb, y + 1 - 2 * yl, 3 - x, 3 - y
    own_c = lax.rem((x + 1) // 2, 2) * 2 + lax.rem((y + 1) // 2, 2)

    def device(x_, y_, z_, h_):
        return {"img": lax.rem(y_, 2) * 2 + h_, "cls": (x_ * Z + z_) * 2 + y_ // 2}

    def slice_of(x_, y_):
        return lax.rem((x_ + 1) // 2, 2) * 2 + lax.rem((y_ + 1) // 2, 2)

    other_core = device(x, y, z, 1 - h)
    along_x = [device(wrap(x + d, X), y, z, h) for d in range(1, 4)]
    along_y = [device(x, wrap(y + d, 4), z, h) for d in range(1, 4)]
    along_z = [device(x, y, wrap(z + d, Z), h) for d in range(1, Z)]
    chips = [(x, y), (xm, y), (x, ym), (xm, ym)]
    same_core = [device(a, b, z, h) for a, b in chips]
    cross_core = [device(a, b, z, 1 - h) for a, b in chips]

    barrier = pltpu.get_barrier_semaphore()
    partners = [other_core] + along_x + along_y + along_z + [same_core[3]] + cross_core[1:]
    for partner in partners:
        pl.semaphore_signal(barrier, inc=1, device_id=partner, device_id_type=MESH)

    fetch = pltpu.make_async_copy(images_hbm, im, local_sem.at[0])
    fetch.start()

    count = [0]
    sent = []

    def new_id():
        count[0] += 1
        return count[0] - 1

    def send(src, dst, ident, to):
        copy = pltpu.make_async_remote_copy(src_ref=src, dst_ref=dst, send_sem=send_sem.at[ident],
                                            recv_sem=recv_sem.at[ident], device_id=to, device_id_type=MESH)
        copy.start()
        sent.append(copy)

    def arrived(dst, ident):
        pltpu.make_async_remote_copy(src_ref=dst, dst_ref=dst, send_sem=send_sem.at[ident],
                                     recv_sem=recv_sem.at[ident], device_id=other_core,
                                     device_id_type=MESH).wait_recv()

    row = lax.broadcasted_iota(jnp.int32, (256, 128), 0)
    lane = lax.broadcasted_iota(jnp.int32, (256, 128), 1)
    column = (row >> 4) & 3
    base = ((((row >> 2) & 3) ^ (3 * (column >> 1))) * 128 + (column >> 1) * 64 + (row >> 6) * 4 + (row & 3))
    for v in range(2):
        start = jnp.where(((column ^ (column >> 1)) & 1) == v, base, -4096)
        for s in range(2):
            for si in range(4):
                goes = start ^ (((si ^ (3 * s)) << 7) | (si << 4))
                for c in range(4):
                    regroup[v * 2 + s, si * 256:si * 256 + 256, c * 128:c * 128 + 128] = jnp.where(
                        goes == lane + c * 128, 1.0, 0.0).astype(BF16)
    for s in range(2):
        strip = refs_ref[:, pl.ds(pl.multiple_of((3 * s + yl * (1 - 2 * s)) * 1024, 1024), 1024)]
        placed = jnp.dot(strip, regroup[lax.rem(yl + h, 2) * 2 + s], preferred_element_type=F32)
        for c in range(4):
            ref_slab[c * 4:c * 4 + 4, s * 128:s * 128 + 128] = placed[:, c * 128:c * 128 + 128]
    zgot[z] = ref_slab[...].astype(BF16)
    meta[0, h, 0:1, :] = jnp.concatenate([noise_ref[...]] * 2, axis=1)
    meta[0, h, 1:5, :] = jnp.concatenate([assign_ref[...].astype(F32)] * 2, axis=1)
    meta[0, h, 5:9, :] = jnp.concatenate([turn_ref[...].astype(F32)] * 2, axis=1)

    pl.semaphore_wait(barrier, len(partners))

    ident_z = [new_id() for _ in range(Z - 1)]
    for d in range(1, Z):
        send(zgot.at[z], zgot.at[z], ident_z[d - 1], along_z[d - 1])

    fetch.wait()
    for hh in range(2):
        for u in range(2):
            for s in range(2):
                at = STRIP[u][s] * 1024
                placed = jnp.dot(im[:, at:at + 1024], regroup[(u ^ hh) * 2 + s], preferred_element_type=F32)
                for c in range(4):
                    blocks[hh, c, u, :, s * 128:s * 128 + 128] = placed[:, c * 128:c * 128 + 128].astype(BF16)
    mine = pl.ds(pl.multiple_of(h * 64, 64), 64)
    theirs = pl.ds(pl.multiple_of((1 - h) * 64, 64), 64)
    ident_im, ident_meta = new_id(), new_id()
    send(blocks.at[1 - h], xall.at[:, :, mine, :], ident_im, other_core)
    send(meta.at[0, h], meta.at[0, h], ident_meta, other_core)
    quad_im = [[new_id() for _ in range(2)] for _ in range(3)]
    quad_meta = [[new_id() for _ in range(2)] for _ in range(3)]
    for e in range(1, 4):
        c = slice_of(*chips[e])
        into = pl.ds(pl.multiple_of(e * 128 + h * 64, 64), 64)
        for k, (hh, to) in enumerate(((h, same_core[e]), (1 - h, cross_core[e]))):
            send(blocks.at[hh, c], xquad.at[:, into, :], quad_im[e - 1][k], to)
            send(meta.at[0, h], meta.at[e, h], quad_meta[e - 1][k], to)
    for c in range(4):
        for u in range(2):
            xall[c, u, mine, :] = blocks[h, c, u]

    for d in range(1, Z):
        arrived(zgot.at[wrap(z - d, Z)], ident_z[d - 1])

    def rows(x_, y_):
        return pl.ds(pl.multiple_of((y_ // 2) * 128 + x_ * 32, 32), 32)

    def region(part_, x_, y_):
        return refs.at[pl.ds(lax.rem(y_, 2) * 4 + part_ * 2, 2), rows(x_, y_), :]

    for q in range(Z):
        piece = zgot[q].astype(F32)
        for b in range(4):
            zline[b, q * 4:q * 4 + 4, :] = piece[b * 4:b * 4 + 4, :]
    for b in range(4):
        refs[yl * 4 + b, rows(x, y), :] = zline[b].astype(BF16)

    first_a, first_b = [new_id() for _ in range(3)], [new_id() for _ in range(3)]
    second_a = [[new_id() for _ in range(3)] for _ in range(4)]
    second_b = [[new_id() for _ in range(3)] for _ in range(4)]
    for d in range(3):
        send(region(0, x, y), region(0, x, y), first_a[d], along_x[d])
        send(region(1, x, y), region(1, x, y), first_b[d], along_y[d])
    for e in range(4):
        xe, ye = wrap(x - e, X), wrap(y - e, 4)
        if e:
            arrived(region(0, xe, y), first_a[e - 1])
        for d in range(3):
            send(region(0, xe, y), region(0, xe, y), second_a[e][d], along_y[d])
        if e:
            arrived(region(1, x, ye), first_b[e - 1])
        for d in range(3):
            send(region(1, x, ye), region(1, x, ye), second_b[e][d], along_x[d])

    swapped = ((row >> 6) & 1) * 128 + ((row >> 7) & 1) * 64 + (row & 3) * 4 + ((row >> 2) & 3)
    swapped = swapped + ((((row >> 4) & 3) ^ (3 * ((row >> 6) & 1)) ^ (3 * ((row >> 7) & 1))) << 4)
    for r, (swap, flips) in enumerate(FORMS):
        for c in range(4):
            goes = (swapped ^ (flips ^ (c << 4))) if swap else (row ^ flips)
            for half in range(2):
                inner[r, c, :, half * 128:half * 128 + 128] = jnp.where(goes == lane + half * 128, 1.0, 0.0).astype(BF16)
    arrived(xall.at[:, :, theirs, :], ident_im)
    for r, (swap, flips) in enumerate(FORMS):
        for u in range(2):
            source = u + swap * h * (1 - 2 * u)
            for c in range(4):
                turned[u * 4 + c, r * 128:r * 128 + 128, :] = jnp.dot(
                    xall[c, source], inner[r, c], preferred_element_type=F32).astype(BF16)
    for e in range(1, 4):
        for k, hh in enumerate((h, 1 - h)):
            into = pl.ds(pl.multiple_of(e * 128 + hh * 64, 64), 64)
            arrived(xquad.at[:, into, :], quad_im[e - 1][k])
            arrived(meta.at[e, hh], quad_meta[e - 1][k])
    for u in range(2):
        xquad[u, 0:128, :] = xall[own_c, u]
    for r, (swap, flips) in enumerate(FORMS):
        for u in range(2):
            source = u + swap * h * (1 - 2 * u)
            full = jnp.dot(xquad[source], inner[r, own_c], preferred_element_type=F32).astype(BF16)
            for e in range(4):
                turned_quad[u, e * 1024 + r * 128:e * 1024 + r * 128 + 128, :] = full[e * 128:e * 128 + 128]

    arrived(meta.at[0, 1 - h], ident_meta)
    kappa = lax.broadcasted_iota(jnp.int32, (K, 128), 0)
    label = (((kappa >> 2) & 31) * 8 + (kappa >> 7) * 4 + (kappa & 3)).astype(F32)
    info = [jnp.where(lane[0:16] < 64, meta[e, 0], meta[e, 1]) for e in range(4)]
    for e in range(4):
        tied = jnp.full((K, 128), -1.0, F32)
        for j in range(4):
            tied = jnp.where(label == info[e][1 + j:2 + j, :], info[e][5 + j:6 + j, :], tied)
        tie[e] = tied
    per_noise = 1.0 / info[0][0:1, :]

    for e in range(4):
        for d in range(3):
            arrived(region(0, wrap(x - e, X), wrap(y - d - 1, 4)), second_a[e][d])
            arrived(region(1, wrap(x - d - 1, X), wrap(y - e, 4)), second_b[e][d])

    square = jnp.zeros((K, 128), F32)
    for b in range(8):
        part_ref = refs[b].astype(F32)
        sq = part_ref * part_ref
        square = square + sq[:, :128] + sq[:, 128:]
    half_norm = 0.5 * jnp.sum(square, axis=1, keepdims=True)
    ident_s = [new_id() for _ in range(4)]
    for g in range(4):
        acc = jnp.zeros((K, 256), F32)
        for b in range(8):
            acc = acc + lax.dot_general(refs[b], turned[b, g * 256:g * 256 + 256, :], (((1,), (1,)), ((), ())),
                                        preferred_element_type=F32)
        own_scores[g] = acc - half_norm
        send(own_scores.at[g], other_scores.at[g], ident_s[g], other_core)
    for g in range(4):
        arrived(other_scores.at[g], ident_s[g])

    @pl.loop(0, 8)
    def _(i):
        chunk = pl.ds(pl.multiple_of(i * 32, 32), 32)
        score = []
        for g in range(4):
            both = own_scores[g, chunk, :] + other_scores[g, chunk, :]
            score += [both[:, :128] * per_noise, both[:, 128:] * per_noise]
        top = score[0]
        for s in score[1:]:
            top = jnp.maximum(top, s)
        total = jnp.exp(score[0] - top)
        for s in score[1:]:
            total = total + jnp.exp(s - top)
        per_class[chunk, :] = top + jnp.log(total)

    value = per_class[...]
    named = tie[0] >= 0.0
    best = jnp.max(jnp.where(named, value, -jnp.inf), axis=0, keepdims=True)
    expo = jnp.where(named, jnp.exp(jnp.where(named, value, best) - best), 0.0)
    weight = (expo / jnp.sum(expo, axis=0, keepdims=True)).astype(BF16).astype(F32)
    for j in range(4):
        wts[0, j:j + 1, :] = jnp.sum(jnp.where(label == info[0][1 + j:2 + j, :], weight, 0.0), axis=0, keepdims=True)
    ident_w = [new_id() for _ in range(3)]
    for e in range(1, 4):
        send(wts.at[0], wts.at[e], ident_w[e - 1], same_core[e])

    def fill(e, weight):
        for r in range(8):
            table[:, e * 1024 + r * 128:e * 1024 + r * 128 + 128] = jnp.where(tie[e] == r, weight, 0.0).astype(BF16)
        return lax.dot_general(jnp.ones((8, 128), BF16), weight.astype(BF16), (((1,), (1,)), ((), ())),
                               preferred_element_type=F32)

    totals = fill(0, weight)
    for u in range(2):
        part[u] = jnp.dot(table[:, 0:1024], turned_quad[u, 0:1024, :], preferred_element_type=F32)
    peak = jnp.max(value, axis=0, keepdims=True)
    evidence = peak + jnp.log(jnp.sum(jnp.exp(value - peak), axis=0, keepdims=True))
    evidence_ref[...] = jnp.where(h == 0, evidence[:, :64], evidence[:, 64:])
    for e in range(1, 4):
        arrived(wts.at[e], ident_w[e - 1])
        weight = jnp.zeros((K, 128), F32)
        for j in range(4):
            weight = jnp.where(label == info[e][1 + j:2 + j, :], wts[e, j:j + 1, :], weight)
        totals = totals + fill(e, weight)
    tot[...] = totals

    def part_rows(yh_, xp_):
        return pl.ds(pl.multiple_of(yh_ * 128 + xp_ * 64, 64), 64)

    across_x, across_y = device(xr, y, z, h), device(x, yr, z, h)
    ident_ty, ident_tx = new_id(), new_id()
    one_a, one_b, two_a, two_b = [new_id(), new_id()], [new_id(), new_id()], new_id(), new_id()
    send(tot, tot_y, ident_ty, across_y)
    part[0] = part[0] + jnp.dot(table[:, 1024:], turned_quad[0, 1024:, :], preferred_element_type=F32)
    send(part.at[0, part_rows(1 - yh, 1 - xp)], got_a.at[0], one_a[0], across_y)
    send(part.at[0, part_rows(1 - yh, xp)], got_a.at[1], one_a[1], across_y)
    part[1] = part[1] + jnp.dot(table[:, 1024:], turned_quad[1, 1024:, :], preferred_element_type=F32)
    send(part.at[1, part_rows(1 - yh, 1 - xp)], got_b.at[0], one_b[0], across_x)
    send(part.at[1, part_rows(yh, 1 - xp)], got_b.at[1], one_b[1], across_x)

    arrived(tot_y, ident_ty)
    lines[...] = tot[...] + tot_y[...]
    send(lines, tot_x, ident_tx, across_x)
    arrived(got_a.at[0], one_a[0])
    onward = part.at[0, part_rows(yh, 1 - xp)]
    onward[...] = onward[...] + got_a[0]
    send(onward, got_a2, two_a, across_x)
    arrived(got_b.at[0], one_b[0])
    onward = part.at[1, part_rows(1 - yh, xp)]
    onward[...] = onward[...] + got_b[0]
    send(onward, got_b2, two_b, across_y)
    arrived(got_a.at[1], one_a[1])
    whole_a = part[0, part_rows(yh, xp), :] + got_a[1]
    arrived(got_b.at[1], one_b[1])
    whole_b = part[1, part_rows(yh, xp), :] + got_b[1]
    arrived(tot_x, ident_tx)
    line = lines[...] + tot_x[...]
    arrived(got_a2, two_a)
    arrived(got_b2, two_b)

    for u, whole in enumerate((whole_a + got_a2[...], whole_b + got_b2[...])):
        for b in range(2):
            for q in range(Z):
                zsend[q, u * 8 + b * 4:u * 8 + b * 4 + 4, :] = whole[b * 32 + q * 4:b * 32 + q * 4 + 4, :]
    for q in range(Z):
        zsend[q, 16:24, :] = line
    ident_zr = [new_id() for _ in range(Z - 1)]
    for d in range(1, Z):
        send(zsend.at[wrap(z + d, Z)], zrecv.at[d - 1], ident_zr[d - 1], along_z[d - 1])
    final = zsend[z]
    for d in range(Z - 1):
        arrived(zrecv.at[d], ident_zr[d])
        final = final + zrecv[d]

    for b in range(2):
        for u in range(2):
            leave[b, u * 4:u * 4 + 4, :] = final[u * 8 + b * 4:u * 8 + b * 4 + 4, :]
    own_slot = own_c * 2 + h
    ident_o = [[new_id() for _ in range(2)] for _ in range(4)]
    send(leave.at[xb], slots.at[own_slot], ident_o[0][1], cross_core[0])
    for e in range(1, 4):
        b = xb + (1 - 2 * xb) * (e % 2)
        send(leave.at[b], slots.at[own_slot], ident_o[e][0], same_core[e])
        send(leave.at[b], slots.at[own_slot], ident_o[e][1], cross_core[e])
    slots[own_slot] = leave[xb]
    place = lax.broadcasted_iota(jnp.int32, (8, 256), 1)
    own_class = yh * 128 + x * 32 + z * 4 + (lax.broadcasted_iota(jnp.int32, (8, 256), 0) & 3)
    total = jnp.sum(jnp.where(place == own_class, jnp.broadcast_to(final[16:17, :], (8, 256)), 0.0), axis=1,
                    keepdims=True)[0:4]
    for e in range(4):
        c = slice_of(*chips[e])
        if e:
            arrived(slots.at[c * 2 + h], ident_o[e][0])
        arrived(slots.at[c * 2 + 1 - h], ident_o[e][1])
    strips = [jnp.zeros((4, 1024), F32) for _ in range(4)]
    for v in range(2):
        for s in range(2):
            for hh in range(2):
                u = v ^ hh
                for c in range(4):
                    zline[c, hh * 4:hh * 4 + 4, 0:128] = slots[c * 2 + hh, u * 4:u * 4 + 4, s * 128:s * 128 + 128]
            left = jnp.concatenate([zline[c, 0:8, 0:128] for c in range(4)], axis=1)
            high = left.astype(BF16).astype(F32)
            middle = (left - high).astype(BF16).astype(F32)
            three = jnp.concatenate([high, middle, left - high - middle], axis=0).astype(BF16)
            placed = lax.dot_general(three, regroup[v * 2 + s], (((1,), (1,)), ((), ())), preferred_element_type=F32)
            placed = placed[0:8] + placed[8:16] + placed[16:24]
            for hh in range(2):
                bi = STRIP[v ^ hh][s]
                strips[bi] = strips[bi] + placed[hh * 4:hh * 4 + 4]
    for bi in range(4):
        at = bi * 1024
        out_ref[:, at:at + 1024] = (strips[bi] + prior_weight * refs_ref[:, at:at + 1024].astype(F32)) / (
            total + prior_weight)

    for copy in sent:
        copy.wait_send()
    assert count[0] <= send_sem.shape[0]


def per_device(images, noise_var, references, assign, rotations):
    count = images.shape[0]
    X, Z = 4, lax.axis_size("cls") // 8
    vmem = pl.BlockSpec(memory_space=pltpu.VMEM)
    out, evidence = pl.pallas_call(
        functools.partial(kernel, X, Z),
        out_shape=(jax.ShapeDtypeStruct((4, SIDE * SIDE), F32), jax.ShapeDtypeStruct((1, count), F32)),
        in_specs=[pl.BlockSpec(memory_space=pltpu.HBM), vmem, vmem, vmem, vmem],
        out_specs=(vmem, vmem),
        scratch_shapes=[
            pltpu.VMEM((count, SIDE * SIDE), BF16),
            pltpu.VMEM((8, 4, 256, 256), BF16),
            pltpu.VMEM((4, 1024, 512), BF16),
            pltpu.VMEM((2, 4, 2, count, 256), BF16),
            pltpu.VMEM((4, 2, 2 * count, 256), BF16),
            pltpu.VMEM((2, 8 * count, 256), BF16),
            pltpu.VMEM((8, 1024, 256), BF16),
            pltpu.VMEM((2, 4096, 256), BF16),
            pltpu.VMEM((4, 2, 16, 128), F32),
            pltpu.VMEM((16, 256), F32),
            pltpu.VMEM((Z, 16, 256), BF16),
            pltpu.VMEM((4, 32, 256), F32),
            pltpu.VMEM((8, K, 256), BF16),
            pltpu.VMEM((4, K, 256), F32),
            pltpu.VMEM((4, K, 256), F32),
            pltpu.VMEM((K, 128), F32),
            pltpu.VMEM((4, K, 128), F32),
            pltpu.VMEM((K, 4096), BF16),
            pltpu.VMEM((2, K, 256), F32),
            pltpu.VMEM((2, 64, 256), F32),
            pltpu.VMEM((2, 64, 256), F32),
            pltpu.VMEM((64, 256), F32),
            pltpu.VMEM((64, 256), F32),
            pltpu.VMEM((4, 8, 128), F32),
            pltpu.VMEM((8, 256), F32),
            pltpu.VMEM((8, 256), F32),
            pltpu.VMEM((8, 256), F32),
            pltpu.VMEM((8, 256), F32),
            pltpu.VMEM((Z, 24, 256), F32),
            pltpu.VMEM((Z - 1, 24, 256), F32),
            pltpu.VMEM((2, 8, 256), F32),
            pltpu.VMEM((8, 8, 256), F32),
            pltpu.SemaphoreType.DMA((1,)),
            pltpu.SemaphoreType.DMA((96,)),
            pltpu.SemaphoreType.DMA((96,)),
        ],
        compiler_params=pltpu.CompilerParams(collective_id=0, has_side_effects=True, vmem_limit_bytes=48 << 20),
        name="classify",
    )(images, references, noise_var[None, :], assign.T, rotations.T)
    return out, evidence[0]


def solution(mesh):
    in_specs = (
        P(("img", "cls"), None),
        P(("img", "cls")),
        P("cls", None),
        P(("img", "cls"), None),
        P(("img", "cls"), None),
    )
    out_specs = (P("cls", None), P(("img", "cls")))
    return jax.shard_map(
        per_device, mesh=mesh, in_specs=in_specs, out_specs=out_specs, check_vma=False
    )
```

```python
import functools

import numpy as np
import jax
import jax.numpy as jnp
from jax import lax
from jax.experimental import pallas as pl
from jax.experimental.pallas import tpu as pltpu
from jax.sharding import PartitionSpec as P

SIDE = 64
K = 256
MESH = pl.DeviceIdType.MESH
F32 = jnp.float32
BF16 = jnp.bfloat16
prior_weight = 16.0

STRIP = ((0, 3), (1, 2))
FLIP_ROWS, FLIP_COLUMNS = 188, 67


def backward_turn(picture, turn):
    quarter = turn % 4
    result = np.rot90(picture, -quarter, axes=(-2, -1))
    return np.swapaxes(result, -1, -2) if turn >= 4 else result


def forms():
    number = np.arange(SIDE * SIDE).reshape(SIDE, SIDE)
    found = []
    for r in range(8):
        source = backward_turn(number, r)
        for swap in (0, 1):
            for rows in (0, 1):
                for columns in (0, 1):
                    trial = number.T if swap else number
                    trial = trial[::-1] if rows else trial
                    trial = trial[:, ::-1] if columns else trial
                    if (trial == source).all():
                        found.append((swap, rows * FLIP_ROWS ^ columns * FLIP_COLUMNS))
    assert len(found) == 8
    return found


FORMS = forms()


def wrap(value, size):
    return lax.rem(value + 2 * size, size)


def kernel(X, Z, images_hbm, refs_hbm, noise_hbm, assign_hbm, turn_hbm, out_ref, evidence_ref,
           im, refs_ref, noise_ref, assign_ref, turn_ref, inner, regroup, blocks, xall, xquad, turned, turned_quad, meta, ref_slab, zgot, zline, refs, own_scores,
           other_scores, per_class, tie, table, part, got_a, got_b, got_a2, got_b2, wts, tot, tot_y, tot_x, lines, all_tot,
           zsend, zrecv, leave, slots, local_sem, send_sem, recv_sem):
    img, cls = lax.axis_index("img"), lax.axis_index("cls")
    yl, h = img // 2, lax.rem(img, 2)
    yh, z, x = lax.rem(cls, 2), lax.rem(cls // 2, Z), cls // (2 * Z)
    y = yh * 2 + yl
    xp, xb = x // 2, lax.rem(x, 2)
    xm, ym, xr, yr = x + 1 - 2 * xb, y + 1 - 2 * yl, 3 - x, 3 - y
    own_c = lax.rem((x + 1) // 2, 2) * 2 + lax.rem((y + 1) // 2, 2)

    def device(x_, y_, z_, h_):
        return {"img": lax.rem(y_, 2) * 2 + h_, "cls": (x_ * Z + z_) * 2 + y_ // 2}

    def slice_of(x_, y_):
        return lax.rem((x_ + 1) // 2, 2) * 2 + lax.rem((y_ + 1) // 2, 2)

    other_core = device(x, y, z, 1 - h)
    along_x = [device(wrap(x + d, X), y, z, h) for d in range(1, 4)]
    along_y = [device(x, wrap(y + d, 4), z, h) for d in range(1, 4)]
    along_z = [device(x, y, wrap(z + d, Z), h) for d in range(1, Z)]
    chips = [(x, y), (xm, y), (x, ym), (xm, ym)]
    same_core = [device(a, b, z, h) for a, b in chips]
    cross_core = [device(a, b, z, 1 - h) for a, b in chips]

    far_first = sorted(range(1, Z), key=lambda d: -min(d, Z - d))

    barrier = pltpu.get_barrier_semaphore()
    partners = [other_core] + along_x + along_y + [same_core[3]] + cross_core[1:] + [along_z[d - 1] for d in far_first[::-1]]
    for partner in reversed(partners):
        pl.semaphore_signal(barrier, inc=1, device_id=partner, device_id_type=MESH)

    fetch = [pltpu.make_async_copy(source, into, local_sem.at[k]) for k, (source, into) in enumerate((
        (refs_hbm, refs_ref), (noise_hbm, noise_ref), (assign_hbm, assign_ref), (turn_hbm, turn_ref), (images_hbm, im)))]
    for copy in fetch:
        copy.start()

    count = [0]
    sent = []

    def new_id():
        count[0] += 1
        return count[0] - 1

    def send(src, dst, ident, to):
        copy = pltpu.make_async_remote_copy(src_ref=src, dst_ref=dst, send_sem=send_sem.at[ident],
                                            recv_sem=recv_sem.at[ident], device_id=to, device_id_type=MESH)
        copy.start()
        sent.append(copy)

    def arrived(dst, ident):
        pltpu.make_async_remote_copy(src_ref=dst, dst_ref=dst, send_sem=send_sem.at[ident],
                                     recv_sem=recv_sem.at[ident], device_id=other_core,
                                     device_id_type=MESH).wait_recv()

    row = lax.broadcasted_iota(jnp.int32, (256, 128), 0)
    lane = lax.broadcasted_iota(jnp.int32, (256, 128), 1)
    column = (row >> 4) & 3
    base = ((((row >> 2) & 3) ^ (3 * (column >> 1))) * 128 + (column >> 1) * 64 + (row >> 6) * 4 + (row & 3))
    for v in range(2):
        start = jnp.where(((column ^ (column >> 1)) & 1) == v, base, -4096)
        for s in range(2):
            for si in range(4):
                goes = start ^ (((si ^ (3 * s)) << 7) | (si << 4))
                for c in range(4):
                    regroup[v * 2 + s, si * 256:si * 256 + 256, c * 128:c * 128 + 128] = jnp.where(
                        goes == lane + c * 128, 1.0, 0.0).astype(BF16)
    for copy in fetch[:4]:
        copy.wait()
    for s in range(2):
        strip = refs_ref[:, pl.ds(pl.multiple_of((3 * s + yl * (1 - 2 * s)) * 1024, 1024), 1024)]
        placed = jnp.dot(strip, regroup[lax.rem(yl + h, 2) * 2 + s], preferred_element_type=F32)
        for c in range(4):
            ref_slab[c * 4:c * 4 + 4, s * 128:s * 128 + 128] = placed[:, c * 128:c * 128 + 128]
    zgot[z] = ref_slab[...].astype(BF16)
    meta[0, h, 0:1, :] = jnp.concatenate([noise_ref[...]] * 2, axis=1)
    meta[0, h, 1:5, :] = jnp.concatenate([assign_ref[...].astype(F32)] * 2, axis=1)
    meta[0, h, 5:9, :] = jnp.concatenate([turn_ref[...].astype(F32)] * 2, axis=1)

    pl.semaphore_wait(barrier, len(partners))

    ident_z = [new_id() for _ in range(Z - 1)]
    for d in far_first:
        send(zgot.at[z], zgot.at[z], ident_z[d - 1], along_z[d - 1])

    fetch[4].wait()
    for hh in range(2):
        for u in range(2):
            for s in range(2):
                at = STRIP[u][s] * 1024
                placed = jnp.dot(im[:, at:at + 1024], regroup[(u ^ hh) * 2 + s], preferred_element_type=F32)
                for c in range(4):
                    blocks[hh, c, u, :, s * 128:s * 128 + 128] = placed[:, c * 128:c * 128 + 128].astype(BF16)
    mine = pl.ds(pl.multiple_of(h * 64, 64), 64)
    theirs = pl.ds(pl.multiple_of((1 - h) * 64, 64), 64)
    ident_im, ident_meta = new_id(), new_id()
    send(blocks.at[1 - h], xall.at[:, :, mine, :], ident_im, other_core)
    send(meta.at[0, h], meta.at[0, h], ident_meta, other_core)
    for c in range(4):
        for u in range(2):
            xall[c, u, mine, :] = blocks[h, c, u]

    for d in range(1, Z):
        arrived(zgot.at[wrap(z - d, Z)], ident_z[d - 1])

    def rows(x_, y_):
        return pl.ds(pl.multiple_of((y_ // 2) * 128 + x_ * 32, 32), 32)

    def region(part_, x_, y_):
        return refs.at[pl.ds(lax.rem(y_, 2) * 4 + part_ * 2, 2), rows(x_, y_), :]

    for q in range(Z):
        piece = zgot[q].astype(F32)
        for b in range(4):
            zline[b, q * 4:q * 4 + 4, :] = piece[b * 4:b * 4 + 4, :]
    for b in range(4):
        refs[yl * 4 + b, rows(x, y), :] = zline[b].astype(BF16)

    first_a, first_b = [new_id() for _ in range(3)], [new_id() for _ in range(3)]
    second_a = [[new_id() for _ in range(3)] for _ in range(4)]
    second_b = [[new_id() for _ in range(3)] for _ in range(4)]
    for d in (1, 0, 2):
        send(region(0, x, y), region(0, x, y), first_a[d], along_x[d])
        send(region(1, x, y), region(1, x, y), first_b[d], along_y[d])
    for e in range(4):
        xe, ye = wrap(x - e, X), wrap(y - e, 4)
        if e:
            arrived(region(0, xe, y), first_a[e - 1])
        for d in (1, 0, 2):
            send(region(0, xe, y), region(0, xe, y), second_a[e][d], along_y[d])
        if e:
            arrived(region(1, x, ye), first_b[e - 1])
        for d in (1, 0, 2):
            send(region(1, x, ye), region(1, x, ye), second_b[e][d], along_x[d])

    swapped = ((row >> 6) & 1) * 128 + ((row >> 7) & 1) * 64 + (row & 3) * 4 + ((row >> 2) & 3)
    swapped = swapped + ((((row >> 4) & 3) ^ (3 * ((row >> 6) & 1)) ^ (3 * ((row >> 7) & 1))) << 4)
    for r, (swap, flips) in enumerate(FORMS):
        for c in range(4):
            goes = (swapped ^ (flips ^ (c << 4))) if swap else (row ^ flips)
            for half in range(2):
                inner[r, c, :, half * 128:half * 128 + 128] = jnp.where(goes == lane + half * 128, 1.0, 0.0).astype(BF16)
    arrived(xall.at[:, :, theirs, :], ident_im)
    for r, (swap, flips) in enumerate(FORMS):
        for u in range(2):
            source = u + swap * h * (1 - 2 * u)
            for c in range(4):
                turned[u * 4 + c, r * 128:r * 128 + 128, :] = jnp.dot(
                    xall[c, source], inner[r, c], preferred_element_type=F32).astype(BF16)
    arrived(meta.at[0, 1 - h], ident_meta)
    kappa = lax.broadcasted_iota(jnp.int32, (K, 128), 0)
    label = (((kappa >> 2) & 31) * 8 + (kappa >> 7) * 4 + (kappa & 3)).astype(F32)

    def tie_up(e):
        info = jnp.where(lane[0:16] < 64, meta[e, 0], meta[e, 1])
        tied = jnp.full((K, 128), -1.0, F32)
        for j in range(4):
            tied = jnp.where(label == info[1 + j:2 + j, :], info[5 + j:6 + j, :], tied)
        tie[e] = tied
        return info

    info = [tie_up(0)]
    per_noise = 1.0 / info[0][0:1, :]

    for e in range(4):
        for d in range(3):
            arrived(region(0, wrap(x - e, X), wrap(y - d - 1, 4)), second_a[e][d])
            arrived(region(1, wrap(x - d - 1, X), wrap(y - e, 4)), second_b[e][d])

    quad_im = [[new_id() for _ in range(2)] for _ in range(3)]
    quad_meta = [[new_id() for _ in range(2)] for _ in range(3)]
    for e in range(1, 4):
        c = slice_of(*chips[e])
        into = pl.ds(pl.multiple_of(e * 128 + h * 64, 64), 64)
        for k, (hh, to) in enumerate(((h, same_core[e]), (1 - h, cross_core[e]))):
            send(blocks.at[hh, c], xquad.at[:, into, :], quad_im[e - 1][k], to)
            send(meta.at[0, h], meta.at[e, h], quad_meta[e - 1][k], to)

    square = jnp.zeros((K, 128), F32)
    for b in range(8):
        part_ref = refs[b].astype(F32)
        sq = part_ref * part_ref
        square = square + sq[:, :128] + sq[:, 128:]
    half_norm = 0.5 * jnp.sum(square, axis=1, keepdims=True)
    ident_s = [new_id() for _ in range(4)]
    for g in range(4):
        acc = jnp.zeros((K, 256), F32)
        for b in range(8):
            acc = acc + lax.dot_general(refs[b], turned[b, g * 256:g * 256 + 256, :], (((1,), (1,)), ((), ())),
                                        preferred_element_type=F32)
        own_scores[g] = acc - half_norm
        send(own_scores.at[g], other_scores.at[g], ident_s[g], other_core)
    for g in range(4):
        arrived(other_scores.at[g], ident_s[g])

    @pl.loop(0, 8)
    def _(i):
        chunk = pl.ds(pl.multiple_of(i * 32, 32), 32)
        score = []
        for g in range(4):
            both = own_scores[g, chunk, :] + other_scores[g, chunk, :]
            score += [both[:, :128] * per_noise, both[:, 128:] * per_noise]
        top = score[0]
        for s in score[1:]:
            top = jnp.maximum(top, s)
        total = jnp.exp(score[0] - top)
        for s in score[1:]:
            total = total + jnp.exp(s - top)
        per_class[chunk, :] = top + jnp.log(total)

    value = per_class[...]
    named = tie[0] >= 0.0
    best = jnp.max(jnp.where(named, value, -jnp.inf), axis=0, keepdims=True)
    expo = jnp.where(named, jnp.exp(jnp.where(named, value, best) - best), 0.0)
    weight = (expo / jnp.sum(expo, axis=0, keepdims=True)).astype(BF16).astype(F32)
    for j in range(4):
        wts[0, j:j + 1, :] = jnp.sum(jnp.where(label == info[0][1 + j:2 + j, :], weight, 0.0), axis=0, keepdims=True)
    ident_w = [new_id() for _ in range(3)]
    for e in range(1, 4):
        send(wts.at[0], wts.at[e], ident_w[e - 1], same_core[e])

    def fill(e, weight):
        for r in range(8):
            table[:, e * 1024 + r * 128:e * 1024 + r * 128 + 128] = jnp.where(tie[e] == r, weight, 0.0).astype(BF16)
        return lax.dot_general(jnp.ones((8, 128), BF16), weight.astype(BF16), (((1,), (1,)), ((), ())),
                               preferred_element_type=F32)[0:1]

    def add(e, u, where):
        more = jnp.dot(table[where, e * 1024:e * 1024 + 1024], turned_quad[u, e * 1024:e * 1024 + 1024, :],
                       preferred_element_type=F32)
        part[u, where] = part[u, where] + more if e else more

    def turn_quad(first, last):
        for r, (swap, flips) in enumerate(FORMS):
            for u in range(2):
                source = u + swap * h * (1 - 2 * u)
                full = jnp.dot(xquad[source, first * 128:last * 128], inner[r, own_c],
                               preferred_element_type=F32).astype(BF16)
                for e in range(first, last):
                    turned_quad[u, e * 1024 + r * 128:e * 1024 + r * 128 + 128, :] = (
                        full[(e - first) * 128:(e - first) * 128 + 128])

    for u in range(2):
        xquad[u, 0:128, :] = xall[own_c, u]
    everything = slice(0, K)
    totals = fill(0, weight)
    turn_quad(0, 1)
    for u in range(2):
        add(0, u, everything)
    for e in range(1, 4):
        for k, hh in enumerate((h, 1 - h)):
            into = pl.ds(pl.multiple_of(e * 128 + hh * 64, 64), 64)
            arrived(xquad.at[:, into, :], quad_im[e - 1][k])
            arrived(meta.at[e, hh], quad_meta[e - 1][k])
    turn_quad(1, 4)
    info += [tie_up(e) for e in range(1, 4)]
    peak = jnp.max(value, axis=0, keepdims=True)
    evidence = peak + jnp.log(jnp.sum(jnp.exp(value - peak), axis=0, keepdims=True))
    evidence_ref[...] = jnp.where(h == 0, evidence[:, :64], evidence[:, 64:])
    for e in range(1, 4):
        arrived(wts.at[e], ident_w[e - 1])
        weight = jnp.zeros((K, 128), F32)
        for j in range(4):
            weight = jnp.where(label == info[e][1 + j:2 + j, :], wts[e, j:j + 1, :], weight)
        totals = totals + fill(e, weight)
        if e < 3:
            for u in range(2):
                add(e, u, everything)
    tot[...] = totals

    def part_rows(yh_, xp_):
        return pl.ds(pl.multiple_of(yh_ * 128 + xp_ * 64, 64), 64)

    across_x, across_y = device(xr, y, z, h), device(x, yr, z, h)
    ident_ty, ident_tx = new_id(), new_id()
    one_a, one_b, two_a, two_b = [new_id(), new_id()], [new_id(), new_id()], new_id(), new_id()
    send(tot, tot_y, ident_ty, across_y)
    add(3, 0, pl.ds(pl.multiple_of((1 - yh) * 128, 128), 128))
    send(part.at[0, part_rows(1 - yh, 1 - xp)], got_a.at[0], one_a[0], across_y)
    send(part.at[0, part_rows(1 - yh, xp)], got_a.at[1], one_a[1], across_y)
    add(3, 1, part_rows(1 - yh, 1 - xp))
    send(part.at[1, part_rows(1 - yh, 1 - xp)], got_b.at[0], one_b[0], across_x)
    add(3, 1, part_rows(yh, 1 - xp))
    send(part.at[1, part_rows(yh, 1 - xp)], got_b.at[1], one_b[1], across_x)
    add(3, 0, pl.ds(pl.multiple_of(yh * 128, 128), 128))
    add(3, 1, part_rows(1 - yh, xp))
    add(3, 1, part_rows(yh, xp))

    arrived(tot_y, ident_ty)
    lines[...] = tot[...] + tot_y[...]
    send(lines, tot_x, ident_tx, across_x)
    arrived(got_a.at[0], one_a[0])
    onward = part.at[0, part_rows(yh, 1 - xp)]
    onward[...] = onward[...] + got_a[0]
    send(onward, got_a2, two_a, across_x)
    arrived(got_b.at[0], one_b[0])
    onward = part.at[1, part_rows(1 - yh, xp)]
    onward[...] = onward[...] + got_b[0]
    send(onward, got_b2, two_b, across_y)
    arrived(got_a.at[1], one_a[1])
    whole_a = part[0, part_rows(yh, xp), :] + got_a[1]
    arrived(got_b.at[1], one_b[1])
    whole_b = part[1, part_rows(yh, xp), :] + got_b[1]
    arrived(tot_x, ident_tx)
    all_tot[z] = lines[...] + tot_x[...]
    ident_zt = [new_id() for _ in range(Z - 1)]
    for d in far_first:
        send(all_tot.at[z], all_tot.at[z], ident_zt[d - 1], along_z[d - 1])
    arrived(got_a2, two_a)
    arrived(got_b2, two_b)

    for u, whole in enumerate((whole_a + got_a2[...], whole_b + got_b2[...])):
        for b in range(2):
            for q in range(Z):
                zsend[q, u * 8 + b * 4:u * 8 + b * 4 + 4, :] = whole[b * 32 + q * 4:b * 32 + q * 4 + 4, :]
    ident_zr = [new_id() for _ in range(Z - 1)]
    for d in far_first:
        send(zsend.at[wrap(z + d, Z)], zrecv.at[d - 1], ident_zr[d - 1], along_z[d - 1])
    final = zsend[z]
    for d in range(Z - 1):
        arrived(zrecv.at[d], ident_zr[d])
        final = final + zrecv[d]

    for b in range(2):
        for u in range(2):
            leave[b, u * 4:u * 4 + 4, :] = final[u * 8 + b * 4:u * 8 + b * 4 + 4, :]
    own_slot = own_c * 2 + h
    ident_o = [[new_id() for _ in range(2)] for _ in range(4)]
    for e in (3, 2, 1):
        b = xb + (1 - 2 * xb) * (e % 2)
        send(leave.at[b], slots.at[own_slot], ident_o[e][1], cross_core[e])
        send(leave.at[b], slots.at[own_slot], ident_o[e][0], same_core[e])
    send(leave.at[xb], slots.at[own_slot], ident_o[0][1], cross_core[0])
    slots[own_slot] = leave[xb]
    place = lax.broadcasted_iota(jnp.int32, (8, 256), 1)
    own_class = yh * 128 + x * 32 + z * 4 + (lax.broadcasted_iota(jnp.int32, (8, 256), 0) & 3)
    for d in range(1, Z):
        arrived(all_tot.at[wrap(z - d, Z)], ident_zt[d - 1])
    line = all_tot[0]
    for q in range(1, Z):
        line = line + all_tot[q]
    total = jnp.sum(jnp.where(place == own_class, jnp.broadcast_to(line, (8, 256)), 0.0), axis=1, keepdims=True)[0:4]
    for e in range(4):
        c = slice_of(*chips[e])
        if e:
            arrived(slots.at[c * 2 + h], ident_o[e][0])
        arrived(slots.at[c * 2 + 1 - h], ident_o[e][1])
    strips = [jnp.zeros((4, 1024), F32) for _ in range(4)]
    for v in range(2):
        for s in range(2):
            for hh in range(2):
                u = v ^ hh
                for c in range(4):
                    zline[c, hh * 4:hh * 4 + 4, 0:128] = slots[c * 2 + hh, u * 4:u * 4 + 4, s * 128:s * 128 + 128]
            left = jnp.concatenate([zline[c, 0:8, 0:128] for c in range(4)], axis=1)
            high = left.astype(BF16).astype(F32)
            middle = (left - high).astype(BF16).astype(F32)
            three = jnp.concatenate([high, middle, left - high - middle], axis=0).astype(BF16)
            placed = lax.dot_general(three, regroup[v * 2 + s], (((1,), (1,)), ((), ())), preferred_element_type=F32)
            placed = placed[0:8] + placed[8:16] + placed[16:24]
            for hh in range(2):
                bi = STRIP[v ^ hh][s]
                strips[bi] = strips[bi] + placed[hh * 4:hh * 4 + 4]
    for bi in range(4):
        at = bi * 1024
        out_ref[:, at:at + 1024] = (strips[bi] + prior_weight * refs_ref[:, at:at + 1024].astype(F32)) / (
            total + prior_weight)

    for copy in sent:
        copy.wait_send()
    assert count[0] <= send_sem.shape[0]


def per_device(images, noise_var, references, assign, rotations):
    count = images.shape[0]
    X, Z = 4, lax.axis_size("cls") // 8
    vmem = pl.BlockSpec(memory_space=pltpu.VMEM)
    out, evidence = pl.pallas_call(
        functools.partial(kernel, X, Z),
        out_shape=(jax.ShapeDtypeStruct((4, SIDE * SIDE), F32), jax.ShapeDtypeStruct((1, count), F32)),
        in_specs=[pl.BlockSpec(memory_space=pl.ANY)] * 5,
        out_specs=(vmem, vmem),
        scratch_shapes=[
            pltpu.VMEM((count, SIDE * SIDE), BF16),
            pltpu.VMEM((4, SIDE * SIDE), BF16),
            pltpu.VMEM((1, count), F32),
            pltpu.VMEM((4, count), jnp.int32),
            pltpu.VMEM((4, count), jnp.int32),
            pltpu.VMEM((8, 4, 256, 256), BF16),
            pltpu.VMEM((4, 1024, 512), BF16),
            pltpu.VMEM((2, 4, 2, count, 256), BF16),
            pltpu.VMEM((4, 2, 2 * count, 256), BF16),
            pltpu.VMEM((2, 8 * count, 256), BF16),
            pltpu.VMEM((8, 1024, 256), BF16),
            pltpu.VMEM((2, 4096, 256), BF16),
            pltpu.VMEM((4, 2, 16, 128), F32),
            pltpu.VMEM((16, 256), F32),
            pltpu.VMEM((Z, 16, 256), BF16),
            pltpu.VMEM((4, 32, 256), F32),
            pltpu.VMEM((8, K, 256), BF16),
            pltpu.VMEM((4, K, 256), F32),
            pltpu.VMEM((4, K, 256), F32),
            pltpu.VMEM((K, 128), F32),
            pltpu.VMEM((4, K, 128), F32),
            pltpu.VMEM((K, 4096), BF16),
            pltpu.VMEM((2, K, 256), F32),
            pltpu.VMEM((2, 64, 256), F32),
            pltpu.VMEM((2, 64, 256), F32),
            pltpu.VMEM((64, 256), F32),
            pltpu.VMEM((64, 256), F32),
            pltpu.VMEM((4, 8, 128), F32),
            pltpu.VMEM((1, 256), F32),
            pltpu.VMEM((1, 256), F32),
            pltpu.VMEM((1, 256), F32),
            pltpu.VMEM((1, 256), F32),
            pltpu.VMEM((Z, 1, 256), F32),
            pltpu.VMEM((Z, 16, 256), F32),
            pltpu.VMEM((Z - 1, 16, 256), F32),
            pltpu.VMEM((2, 8, 256), F32),
            pltpu.VMEM((8, 8, 256), F32),
            pltpu.SemaphoreType.DMA((5,)),
            pltpu.SemaphoreType.DMA((96,)),
            pltpu.SemaphoreType.DMA((96,)),
        ],
        compiler_params=pltpu.CompilerParams(collective_id=0, has_side_effects=True, vmem_limit_bytes=60 << 20),
        name="classify",
    )(images, references, noise_var[None, :], assign.T, rotations.T)
    return out, evidence[0]


def solution(mesh):
    in_specs = (
        P(("img", "cls"), None),
        P(("img", "cls")),
        P("cls", None),
        P(("img", "cls"), None),
        P(("img", "cls"), None),
    )
    out_specs = (P("cls", None), P(("img", "cls")))
    return jax.shard_map(
        per_device, mesh=mesh, in_specs=in_specs, out_specs=out_specs, check_vma=False
    )
```

```python
import functools

import numpy as np
import jax
import jax.numpy as jnp
from jax import lax
from jax.experimental import pallas as pl
from jax.experimental.pallas import tpu as pltpu
from jax.sharding import PartitionSpec as P

SIDE = 64
K = 256
MESH = pl.DeviceIdType.MESH
F32 = jnp.float32
BF16 = jnp.bfloat16
prior_weight = 16.0

STRIP = ((0, 3), (1, 2))
FLIP_ROWS, FLIP_COLUMNS = 188, 67


def backward_turn(picture, turn):
    quarter = turn % 4
    result = np.rot90(picture, -quarter, axes=(-2, -1))
    return np.swapaxes(result, -1, -2) if turn >= 4 else result


def forms():
    number = np.arange(SIDE * SIDE).reshape(SIDE, SIDE)
    found = []
    for r in range(8):
        source = backward_turn(number, r)
        for swap in (0, 1):
            for rows in (0, 1):
                for columns in (0, 1):
                    trial = number.T if swap else number
                    trial = trial[::-1] if rows else trial
                    trial = trial[:, ::-1] if columns else trial
                    if (trial == source).all():
                        found.append((swap, rows * FLIP_ROWS ^ columns * FLIP_COLUMNS))
    assert len(found) == 8
    return found


FORMS = forms()


def wrap(value, size):
    return lax.rem(value + 2 * size, size)


def kernel(X, Z, images_hbm, refs_hbm, noise_hbm, assign_hbm, turn_hbm, out_ref, evidence_ref,
           im, refs_ref, noise_ref, assign_ref, turn_ref, inner, regroup, blocks, xall, xquad, turned, turned_quad, meta, ref_slab, zgot, zline, refs, own_scores,
           other_scores, per_class, tie, table, part, got_a, got_b, got_a2, got_b2, wts, tot, tot_y, tot_x, lines, all_tot,
           zsend, zrecv, leave, slots, local_sem, send_sem, recv_sem):
    img, cls = lax.axis_index("img"), lax.axis_index("cls")
    yl, h = img // 2, lax.rem(img, 2)
    yh, z, x = lax.rem(cls, 2), lax.rem(cls // 2, Z), cls // (2 * Z)
    y = yh * 2 + yl
    xp, xb = x // 2, lax.rem(x, 2)
    xm, ym, xr, yr = x + 1 - 2 * xb, y + 1 - 2 * yl, 3 - x, 3 - y
    own_c = lax.rem((x + 1) // 2, 2) * 2 + lax.rem((y + 1) // 2, 2)

    def device(x_, y_, z_, h_):
        return {"img": lax.rem(y_, 2) * 2 + h_, "cls": (x_ * Z + z_) * 2 + y_ // 2}

    def slice_of(x_, y_):
        return lax.rem((x_ + 1) // 2, 2) * 2 + lax.rem((y_ + 1) // 2, 2)

    other_core = device(x, y, z, 1 - h)
    along_x = [device(wrap(x + d, X), y, z, h) for d in range(1, 4)]
    along_y = [device(x, wrap(y + d, 4), z, h) for d in range(1, 4)]
    along_z = [device(x, y, wrap(z + d, Z), h) for d in range(1, Z)]
    chips = [(x, y), (xm, y), (x, ym), (xm, ym)]
    same_core = [device(a, b, z, h) for a, b in chips]
    cross_core = [device(a, b, z, 1 - h) for a, b in chips]

    far_first = sorted(range(1, Z), key=lambda d: -min(d, Z - d))

    barrier = pltpu.get_barrier_semaphore()
    partners = [other_core] + along_x + along_y + [same_core[3]] + cross_core[1:] + [along_z[d - 1] for d in far_first[::-1]]
    for partner in reversed(partners):
        pl.semaphore_signal(barrier, inc=1, device_id=partner, device_id_type=MESH)

    fetch = [pltpu.make_async_copy(source, into, local_sem.at[k]) for k, (source, into) in enumerate((
        (refs_hbm, refs_ref), (noise_hbm, noise_ref), (assign_hbm, assign_ref), (turn_hbm, turn_ref), (images_hbm, im)))]
    for copy in fetch:
        copy.start()

    count = [0]
    sent = []

    def new_id():
        count[0] += 1
        return count[0] - 1

    def send(src, dst, ident, to):
        copy = pltpu.make_async_remote_copy(src_ref=src, dst_ref=dst, send_sem=send_sem.at[ident],
                                            recv_sem=recv_sem.at[ident], device_id=to, device_id_type=MESH)
        copy.start()
        sent.append(copy)

    def arrived(dst, ident):
        pltpu.make_async_remote_copy(src_ref=dst, dst_ref=dst, send_sem=send_sem.at[ident],
                                     recv_sem=recv_sem.at[ident], device_id=other_core,
                                     device_id_type=MESH).wait_recv()

    row = lax.broadcasted_iota(jnp.int32, (256, 128), 0)
    lane = lax.broadcasted_iota(jnp.int32, (256, 128), 1)
    column = (row >> 4) & 3
    base = ((((row >> 2) & 3) ^ (3 * (column >> 1))) * 128 + (column >> 1) * 64 + (row >> 6) * 4 + (row & 3))
    for v in range(2):
        start = jnp.where(((column ^ (column >> 1)) & 1) == v, base, -4096)
        for s in range(2):
            for si in range(4):
                goes = start ^ (((si ^ (3 * s)) << 7) | (si << 4))
                for c in range(4):
                    regroup[v * 2 + s, si * 256:si * 256 + 256, c * 128:c * 128 + 128] = jnp.where(
                        goes == lane + c * 128, 1.0, 0.0).astype(BF16)
    for copy in fetch[:4]:
        copy.wait()
    for s in range(2):
        strip = refs_ref[:, pl.ds(pl.multiple_of((3 * s + yl * (1 - 2 * s)) * 1024, 1024), 1024)]
        placed = jnp.dot(strip, regroup[lax.rem(yl + h, 2) * 2 + s], preferred_element_type=F32)
        for c in range(4):
            ref_slab[c * 4:c * 4 + 4, s * 128:s * 128 + 128] = placed[:, c * 128:c * 128 + 128]
    zgot[z] = ref_slab[...].astype(BF16)
    meta[0, h, 0:1, :] = jnp.concatenate([noise_ref[...]] * 2, axis=1)
    meta[0, h, 1:5, :] = jnp.concatenate([assign_ref[...].astype(F32)] * 2, axis=1)
    meta[0, h, 5:9, :] = jnp.concatenate([turn_ref[...].astype(F32)] * 2, axis=1)

    pl.semaphore_wait(barrier, len(partners))

    ident_z = [new_id() for _ in range(Z - 1)]
    for d in far_first:
        send(zgot.at[z], zgot.at[z], ident_z[d - 1], along_z[d - 1])

    fetch[4].wait()
    for hh in range(2):
        for u in range(2):
            for s in range(2):
                at = STRIP[u][s] * 1024
                placed = jnp.dot(im[:, at:at + 1024], regroup[(u ^ hh) * 2 + s], preferred_element_type=F32)
                for c in range(4):
                    blocks[hh, c, u, :, s * 128:s * 128 + 128] = placed[:, c * 128:c * 128 + 128].astype(BF16)
    mine = pl.ds(pl.multiple_of(h * 64, 64), 64)
    theirs = pl.ds(pl.multiple_of((1 - h) * 64, 64), 64)
    ident_im, ident_meta = new_id(), new_id()
    send(blocks.at[1 - h], xall.at[:, :, mine, :], ident_im, other_core)
    send(meta.at[0, h], meta.at[0, h], ident_meta, other_core)
    for c in range(4):
        for u in range(2):
            xall[c, u, mine, :] = blocks[h, c, u]

    for d in range(1, Z):
        arrived(zgot.at[wrap(z - d, Z)], ident_z[d - 1])

    def rows(x_, y_):
        return pl.ds(pl.multiple_of((y_ // 2) * 128 + x_ * 32, 32), 32)

    def region(part_, x_, y_):
        return refs.at[pl.ds(lax.rem(y_, 2) * 4 + part_ * 2, 2), rows(x_, y_), :]

    for q in range(Z):
        piece = zgot[q].astype(F32)
        for b in range(4):
            zline[b, q * 4:q * 4 + 4, :] = piece[b * 4:b * 4 + 4, :]
    for b in range(4):
        refs[yl * 4 + b, rows(x, y), :] = zline[b].astype(BF16)

    first_a, first_b = [new_id() for _ in range(3)], [new_id() for _ in range(3)]
    second_a = [[new_id() for _ in range(3)] for _ in range(4)]
    second_b = [[new_id() for _ in range(3)] for _ in range(4)]
    for d in (1, 0, 2):
        send(region(0, x, y), region(0, x, y), first_a[d], along_x[d])
        send(region(1, x, y), region(1, x, y), first_b[d], along_y[d])
    for e in range(4):
        xe, ye = wrap(x - e, X), wrap(y - e, 4)
        if e:
            arrived(region(0, xe, y), first_a[e - 1])
        for d in (1, 0, 2):
            send(region(0, xe, y), region(0, xe, y), second_a[e][d], along_y[d])
        if e:
            arrived(region(1, x, ye), first_b[e - 1])
        for d in (1, 0, 2):
            send(region(1, x, ye), region(1, x, ye), second_b[e][d], along_x[d])

    swapped = ((row >> 6) & 1) * 128 + ((row >> 7) & 1) * 64 + (row & 3) * 4 + ((row >> 2) & 3)
    swapped = swapped + ((((row >> 4) & 3) ^ (3 * ((row >> 6) & 1)) ^ (3 * ((row >> 7) & 1))) << 4)
    for r, (swap, flips) in enumerate(FORMS):
        for c in range(4):
            goes = (swapped ^ (flips ^ (c << 4))) if swap else (row ^ flips)
            for half in range(2):
                inner[r, c, :, half * 128:half * 128 + 128] = jnp.where(goes == lane + half * 128, 1.0, 0.0).astype(BF16)
    arrived(xall.at[:, :, theirs, :], ident_im)
    for r, (swap, flips) in enumerate(FORMS):
        for u in range(2):
            source = u + swap * h * (1 - 2 * u)
            for c in range(4):
                turned[u * 4 + c, r * 128:r * 128 + 128, :] = jnp.dot(
                    xall[c, source], inner[r, c], preferred_element_type=F32).astype(BF16)
    arrived(meta.at[0, 1 - h], ident_meta)
    kappa = lax.broadcasted_iota(jnp.int32, (K, 128), 0)
    label = (((kappa >> 2) & 31) * 8 + (kappa >> 7) * 4 + (kappa & 3)).astype(F32)

    def tie_up(e):
        info = jnp.where(lane[0:16] < 64, meta[e, 0], meta[e, 1])
        tied = jnp.full((K, 128), -1.0, F32)
        for j in range(4):
            tied = jnp.where(label == info[1 + j:2 + j, :], info[5 + j:6 + j, :], tied)
        tie[e] = tied
        return info

    info = [tie_up(0)]
    per_noise = 1.0 / info[0][0:1, :]

    for e in range(4):
        for d in range(3):
            arrived(region(0, wrap(x - e, X), wrap(y - d - 1, 4)), second_a[e][d])
            arrived(region(1, wrap(x - d - 1, X), wrap(y - e, 4)), second_b[e][d])

    quad_im = [[new_id() for _ in range(2)] for _ in range(3)]
    quad_meta = [[new_id() for _ in range(2)] for _ in range(3)]
    for e in (3, 2, 1):
        c = slice_of(*chips[e])
        into = pl.ds(pl.multiple_of(e * 128 + h * 64, 64), 64)
        for k, (hh, to) in enumerate(((h, same_core[e]), (1 - h, cross_core[e]))):
            send(blocks.at[hh, c], xquad.at[:, into, :], quad_im[e - 1][k], to)
            send(meta.at[0, h], meta.at[e, h], quad_meta[e - 1][k], to)

    square = jnp.zeros((K, 128), F32)
    for b in range(8):
        part_ref = refs[b].astype(F32)
        sq = part_ref * part_ref
        square = square + sq[:, :128] + sq[:, 128:]
    half_norm = 0.5 * jnp.sum(square, axis=1, keepdims=True)
    ident_s = [new_id() for _ in range(4)]
    for g in range(4):
        acc = jnp.zeros((K, 256), F32)
        for b in range(8):
            acc = acc + lax.dot_general(refs[b], turned[b, g * 256:g * 256 + 256, :], (((1,), (1,)), ((), ())),
                                        preferred_element_type=F32)
        own_scores[g] = acc - half_norm
        send(own_scores.at[g], other_scores.at[g], ident_s[g], other_core)
    for g in range(4):
        arrived(other_scores.at[g], ident_s[g])

    @pl.loop(0, 8)
    def _(i):
        chunk = pl.ds(pl.multiple_of(i * 32, 32), 32)
        score = []
        for g in range(4):
            both = own_scores[g, chunk, :] + other_scores[g, chunk, :]
            score += [both[:, :128] * per_noise, both[:, 128:] * per_noise]
        top = score[0]
        for s in score[1:]:
            top = jnp.maximum(top, s)
        total = jnp.exp(score[0] - top)
        for s in score[1:]:
            total = total + jnp.exp(s - top)
        per_class[chunk, :] = top + jnp.log(total)

    value = per_class[...]
    named = tie[0] >= 0.0
    best = jnp.max(jnp.where(named, value, -jnp.inf), axis=0, keepdims=True)
    expo = jnp.where(named, jnp.exp(jnp.where(named, value, best) - best), 0.0)
    weight = (expo / jnp.sum(expo, axis=0, keepdims=True)).astype(BF16).astype(F32)
    for j in range(4):
        wts[0, j:j + 1, :] = jnp.sum(jnp.where(label == info[0][1 + j:2 + j, :], weight, 0.0), axis=0, keepdims=True)
    ident_w = [new_id() for _ in range(3)]
    for e in range(1, 4):
        send(wts.at[0], wts.at[e], ident_w[e - 1], same_core[e])

    def fill(e, weight):
        for r in range(8):
            table[:, e * 1024 + r * 128:e * 1024 + r * 128 + 128] = jnp.where(tie[e] == r, weight, 0.0).astype(BF16)
        return lax.dot_general(jnp.ones((8, 128), BF16), weight.astype(BF16), (((1,), (1,)), ((), ())),
                               preferred_element_type=F32)[0:1]

    def add(e, u, where):
        more = jnp.dot(table[where, e * 1024:e * 1024 + 1024], turned_quad[u, e * 1024:e * 1024 + 1024, :],
                       preferred_element_type=F32)
        part[u, where] = part[u, where] + more if e else more

    def turn_quad(first, last):
        for r, (swap, flips) in enumerate(FORMS):
            for u in range(2):
                source = u + swap * h * (1 - 2 * u)
                full = jnp.dot(xquad[source, first * 128:last * 128], inner[r, own_c],
                               preferred_element_type=F32).astype(BF16)
                for e in range(first, last):
                    turned_quad[u, e * 1024 + r * 128:e * 1024 + r * 128 + 128, :] = (
                        full[(e - first) * 128:(e - first) * 128 + 128])

    for u in range(2):
        xquad[u, 0:128, :] = xall[own_c, u]
    everything = slice(0, K)
    totals = fill(0, weight)
    turn_quad(0, 1)
    for u in range(2):
        add(0, u, everything)
    for e in range(1, 4):
        for k, hh in enumerate((h, 1 - h)):
            into = pl.ds(pl.multiple_of(e * 128 + hh * 64, 64), 64)
            arrived(xquad.at[:, into, :], quad_im[e - 1][k])
            arrived(meta.at[e, hh], quad_meta[e - 1][k])
    turn_quad(1, 4)
    info += [tie_up(e) for e in range(1, 4)]
    peak = jnp.max(value, axis=0, keepdims=True)
    evidence = peak + jnp.log(jnp.sum(jnp.exp(value - peak), axis=0, keepdims=True))
    evidence_ref[...] = jnp.where(h == 0, evidence[:, :64], evidence[:, 64:])
    for e in range(1, 4):
        arrived(wts.at[e], ident_w[e - 1])
        weight = jnp.zeros((K, 128), F32)
        for j in range(4):
            weight = jnp.where(label == info[e][1 + j:2 + j, :], wts[e, j:j + 1, :], weight)
        totals = totals + fill(e, weight)
        if e < 3:
            for u in range(2):
                add(e, u, everything)
    tot[...] = totals

    def part_rows(yh_, xp_):
        return pl.ds(pl.multiple_of(yh_ * 128 + xp_ * 64, 64), 64)

    across_x, across_y = device(xr, y, z, h), device(x, yr, z, h)
    ident_ty, ident_tx = new_id(), new_id()
    one_a, one_b, two_a, two_b = [new_id(), new_id()], [new_id(), new_id()], new_id(), new_id()
    send(tot, tot_y, ident_ty, across_y)
    add(3, 0, pl.ds(pl.multiple_of((1 - yh) * 128, 128), 128))
    send(part.at[0, part_rows(1 - yh, 1 - xp)], got_a.at[0], one_a[0], across_y)
    send(part.at[0, part_rows(1 - yh, xp)], got_a.at[1], one_a[1], across_y)
    add(3, 1, part_rows(1 - yh, 1 - xp))
    send(part.at[1, part_rows(1 - yh, 1 - xp)], got_b.at[0], one_b[0], across_x)
    add(3, 1, part_rows(yh, 1 - xp))
    send(part.at[1, part_rows(yh, 1 - xp)], got_b.at[1], one_b[1], across_x)
    add(3, 0, pl.ds(pl.multiple_of(yh * 128, 128), 128))
    add(3, 1, part_rows(1 - yh, xp))
    add(3, 1, part_rows(yh, xp))

    arrived(tot_y, ident_ty)
    lines[...] = tot[...] + tot_y[...]
    send(lines, tot_x, ident_tx, across_x)
    arrived(got_a.at[0], one_a[0])
    onward = part.at[0, part_rows(yh, 1 - xp)]
    onward[...] = onward[...] + got_a[0]
    send(onward, got_a2, two_a, across_x)
    arrived(got_b.at[0], one_b[0])
    onward = part.at[1, part_rows(1 - yh, xp)]
    onward[...] = onward[...] + got_b[0]
    send(onward, got_b2, two_b, across_y)
    arrived(got_a.at[1], one_a[1])
    whole_a = part[0, part_rows(yh, xp), :] + got_a[1]
    arrived(got_b.at[1], one_b[1])
    whole_b = part[1, part_rows(yh, xp), :] + got_b[1]
    arrived(tot_x, ident_tx)
    all_tot[z] = lines[...] + tot_x[...]
    ident_zt = [new_id() for _ in range(Z - 1)]
    for d in far_first:
        send(all_tot.at[z], all_tot.at[z], ident_zt[d - 1], along_z[d - 1])
    arrived(got_a2, two_a)
    arrived(got_b2, two_b)

    for u, whole in enumerate((whole_a + got_a2[...], whole_b + got_b2[...])):
        for b in range(2):
            for q in range(Z):
                zsend[q, u * 8 + b * 4:u * 8 + b * 4 + 4, :] = whole[b * 32 + q * 4:b * 32 + q * 4 + 4, :]
    ident_zr = [new_id() for _ in range(Z - 1)]
    for d in far_first:
        send(zsend.at[wrap(z + d, Z)], zrecv.at[d - 1], ident_zr[d - 1], along_z[d - 1])
    final = zsend[z]
    for d in range(Z - 1):
        arrived(zrecv.at[d], ident_zr[d])
        final = final + zrecv[d]

    for b in range(2):
        for u in range(2):
            leave[b, u * 4:u * 4 + 4, :] = final[u * 8 + b * 4:u * 8 + b * 4 + 4, :]
    own_slot = own_c * 2 + h
    ident_o = [[new_id() for _ in range(2)] for _ in range(4)]
    for e in (3, 2, 1):
        b = xb + (1 - 2 * xb) * (e % 2)
        send(leave.at[b], slots.at[own_slot], ident_o[e][1], cross_core[e])
        send(leave.at[b], slots.at[own_slot], ident_o[e][0], same_core[e])
    send(leave.at[xb], slots.at[own_slot], ident_o[0][1], cross_core[0])
    slots[own_slot] = leave[xb]
    place = lax.broadcasted_iota(jnp.int32, (8, 256), 1)
    own_class = yh * 128 + x * 32 + z * 4 + (lax.broadcasted_iota(jnp.int32, (8, 256), 0) & 3)
    for d in range(1, Z):
        arrived(all_tot.at[wrap(z - d, Z)], ident_zt[d - 1])
    line = all_tot[0]
    for q in range(1, Z):
        line = line + all_tot[q]
    total = jnp.sum(jnp.where(place == own_class, jnp.broadcast_to(line, (8, 256)), 0.0), axis=1, keepdims=True)[0:4]
    for e in range(4):
        c = slice_of(*chips[e])
        if e:
            arrived(slots.at[c * 2 + h], ident_o[e][0])
        arrived(slots.at[c * 2 + 1 - h], ident_o[e][1])
    strips = [jnp.zeros((4, 1024), F32) for _ in range(4)]
    for v in range(2):
        for s in range(2):
            for hh in range(2):
                u = v ^ hh
                for c in range(4):
                    zline[c, hh * 4:hh * 4 + 4, 0:128] = slots[c * 2 + hh, u * 4:u * 4 + 4, s * 128:s * 128 + 128]
            left = jnp.concatenate([zline[c, 0:8, 0:128] for c in range(4)], axis=1)
            high = left.astype(BF16).astype(F32)
            middle = (left - high).astype(BF16).astype(F32)
            three = jnp.concatenate([high, middle, left - high - middle], axis=0).astype(BF16)
            placed = lax.dot_general(three, regroup[v * 2 + s], (((1,), (1,)), ((), ())), preferred_element_type=F32)
            placed = placed[0:8] + placed[8:16] + placed[16:24]
            for hh in range(2):
                bi = STRIP[v ^ hh][s]
                strips[bi] = strips[bi] + placed[hh * 4:hh * 4 + 4]
    for bi in range(4):
        at = bi * 1024
        out_ref[:, at:at + 1024] = (strips[bi] + prior_weight * refs_ref[:, at:at + 1024].astype(F32)) / (
            total + prior_weight)

    for copy in sent:
        copy.wait_send()
    assert count[0] <= send_sem.shape[0]


def per_device(images, noise_var, references, assign, rotations):
    count = images.shape[0]
    X, Z = 4, lax.axis_size("cls") // 8
    vmem = pl.BlockSpec(memory_space=pltpu.VMEM)
    out, evidence = pl.pallas_call(
        functools.partial(kernel, X, Z),
        out_shape=(jax.ShapeDtypeStruct((4, SIDE * SIDE), F32), jax.ShapeDtypeStruct((1, count), F32)),
        in_specs=[pl.BlockSpec(memory_space=pl.ANY)] * 5,
        out_specs=(vmem, vmem),
        scratch_shapes=[
            pltpu.VMEM((count, SIDE * SIDE), BF16),
            pltpu.VMEM((4, SIDE * SIDE), BF16),
            pltpu.VMEM((1, count), F32),
            pltpu.VMEM((4, count), jnp.int32),
            pltpu.VMEM((4, count), jnp.int32),
            pltpu.VMEM((8, 4, 256, 256), BF16),
            pltpu.VMEM((4, 1024, 512), BF16),
            pltpu.VMEM((2, 4, 2, count, 256), BF16),
            pltpu.VMEM((4, 2, 2 * count, 256), BF16),
            pltpu.VMEM((2, 8 * count, 256), BF16),
            pltpu.VMEM((8, 1024, 256), BF16),
            pltpu.VMEM((2, 4096, 256), BF16),
            pltpu.VMEM((4, 2, 16, 128), F32),
            pltpu.VMEM((16, 256), F32),
            pltpu.VMEM((Z, 16, 256), BF16),
            pltpu.VMEM((4, 32, 256), F32),
            pltpu.VMEM((8, K, 256), BF16),
            pltpu.VMEM((4, K, 256), F32),
            pltpu.VMEM((4, K, 256), F32),
            pltpu.VMEM((K, 128), F32),
            pltpu.VMEM((4, K, 128), F32),
            pltpu.VMEM((K, 4096), BF16),
            pltpu.VMEM((2, K, 256), F32),
            pltpu.VMEM((2, 64, 256), F32),
            pltpu.VMEM((2, 64, 256), F32),
            pltpu.VMEM((64, 256), F32),
            pltpu.VMEM((64, 256), F32),
            pltpu.VMEM((4, 8, 128), F32),
            pltpu.VMEM((1, 256), F32),
            pltpu.VMEM((1, 256), F32),
            pltpu.VMEM((1, 256), F32),
            pltpu.VMEM((1, 256), F32),
            pltpu.VMEM((Z, 1, 256), F32),
            pltpu.VMEM((Z, 16, 256), F32),
            pltpu.VMEM((Z - 1, 16, 256), F32),
            pltpu.VMEM((2, 8, 256), F32),
            pltpu.VMEM((8, 8, 256), F32),
            pltpu.SemaphoreType.DMA((5,)),
            pltpu.SemaphoreType.DMA((96,)),
            pltpu.SemaphoreType.DMA((96,)),
        ],
        compiler_params=pltpu.CompilerParams(collective_id=0, has_side_effects=True, vmem_limit_bytes=60 << 20),
        name="classify",
    )(images, references, noise_var[None, :], assign.T, rotations.T)
    return out, evidence[0]


def solution(mesh):
    in_specs = (
        P(("img", "cls"), None),
        P(("img", "cls")),
        P("cls", None),
        P(("img", "cls"), None),
        P(("img", "cls"), None),
    )
    out_specs = (P("cls", None), P(("img", "cls")))
    return jax.shard_map(
        per_device, mesh=mesh, in_specs=in_specs, out_specs=out_specs, check_vma=False
    )
```
